256 devices in a mesh: fsdp: 64 (over z, y, core), rep: 4 (over x).
Axes of the slice: x: 4, y: 4, z: 8, core: 2. Of those that a mesh axis runs over, the one named last changes fastest.
Arguments:
- gradients: bfloat16 [4, 8, 512, 20480], P('rep', None, 'fsdp'), may hold values from -6 to 6
- second_moment: float32 [8, 512, 20480], P(None, 'fsdp', 'rep')
- left_roots: float32 [64, 3, 4, 512, 512], P('fsdp', None, 'rep')
- right_roots: float32 [64, 3, 4, 512, 512], P('fsdp', None, 'rep')
- owners: int32 [320], replicated, may hold values from 0 to 63, as said below
Outputs:
- update: bfloat16 [8, 512, 20480], P(None, 'fsdp')
The draws below stay inside these ranges and needn't reach their ends.
Inputs may be any that keep to these rules, and one draw needn't show every extreme that they name: `owners`: an owner's blocks take its slots 0, 1, 2 ... in increasing block order; every owner holds 1 to 12 blocks, and some owner exactly 12.
All inputs are finite; a program needn't handle non-finite values.
Results may differ from the reference program's by a relative error of at most 0.015.
Values may be sent and summed in bfloat16 or wider, within the bound.
A program may use at most 128 MiB of HBM per device.

```python
import math
import jax
import jax.numpy as jnp
from jax import lax

BS = 512
SLOT_REP = 3
NBR = 8
CW = 20480
NBLK = 320
N_FSDP = 64
N_REP = 4


def draw_owners(key, part):
    key = jax.random.fold_in(key, 11)
    first_key, second_key, third_key = jax.random.split(key, 3)
    patterns = jnp.array([[12, 9, 7, 4, 3, 2, 2, 1], [12, 6, 6, 5, 5, 3, 2, 1], [12, 10, 4, 4, 4, 3, 2, 1]], jnp.int32)
    group_count = N_FSDP // 8
    picks = jax.random.randint(first_key, (group_count,), 0, 3)
    counts = patterns[picks]
    bounds = jnp.cumsum(counts, axis=1).astype(jnp.int32)
    positions = jnp.arange(NBLK, dtype=jnp.int32)
    groups = positions // 40
    offsets = positions % 40
    within = jnp.sum((offsets[:, None] >= bounds[groups]).astype(jnp.int32), axis=1)
    owner_perm = jax.random.permutation(second_key, N_FSDP).astype(jnp.int32)
    owner_list = owner_perm[groups * 8 + within]
    block_perm = jax.random.permutation(third_key, NBLK).astype(jnp.int32)
    table = jnp.zeros((NBLK,), jnp.int32).at[block_perm].set(owner_list)
    return table.astype(jnp.int32)


def root_factor(key):
    diag_key, off_key = jax.random.split(key)
    shape = (N_FSDP, SLOT_REP, N_REP, BS, BS)
    diagonal = jnp.exp(jax.random.uniform(diag_key, shape[:-1], jnp.float32, math.log(0.5), math.log(2.0)))
    spread = jnp.clip(jax.random.normal(off_key, shape, jnp.float32), -4.0, 4.0) * (0.5 / math.sqrt(BS))
    symmetric = (spread + jnp.swapaxes(spread, -1, -2)) * 0.70710678
    rows = jnp.arange(BS, dtype=jnp.int32)
    identity = (rows[:, None] == rows[None, :]).astype(jnp.float32)
    return symmetric * (1.0 - identity) + diagonal[..., None] * identity


def draw_left_roots(key, part):
    key = jax.random.fold_in(key, 21)
    return root_factor(key)


def draw_right_roots(key, part):
    key = jax.random.fold_in(key, 22)
    return root_factor(key)


def draw_second_moment(key, part):
    key = jax.random.fold_in(key, 31)
    column_key, entry_key = jax.random.split(key)
    entries = jnp.exp(jax.random.uniform(entry_key, (NBR, BS, CW), jnp.float32, math.log(0.5), math.log(2.0)))
    rows = jnp.arange(BS, dtype=jnp.float32) / BS
    row_scale = jnp.exp(math.log(10.0) * rows)
    column_scale = jnp.exp(math.log(10.0) * jax.random.uniform(column_key, (CW,), jnp.float32, 0.0, 1.0))
    return 0.01 * row_scale[None, :, None] * column_scale[None, None, :] * entries


def steps_of(own_key, shape, cuts, smallest, largest):
    level, own = 1.0, jax.random.fold_in(own_key, 6)
    for axis_at, parts in cuts:
        steps = jnp.exp(jax.random.uniform(jax.random.fold_in(own, axis_at), (parts,), jnp.float32, smallest / len(cuts), largest / len(cuts)))
        level = level * jnp.repeat(steps, shape[axis_at] // parts).reshape([-1 if axis == axis_at else 1 for axis in range(len(shape))])
    return level


def bell_draw(key, shape, width, limit, pieces=(), kind=jnp.bfloat16):
    drawn = width * jax.random.normal(key, shape, jnp.float32)
    if pieces:
        drawn = drawn * steps_of(key, shape, pieces, -0.22, 0.18)
    return jnp.clip(drawn, -limit, limit).astype(kind)


def setup_inputs(seed: int = 0) -> dict:
    splits = jax.random.split(jax.random.key(seed), 6)
    gradients = bell_draw(splits[0], (N_REP, NBR, BS, CW), 1.0, 6.0, ((0, 4), (2, 64)))
    second_moment = draw_second_moment(jax.random.fold_in(splits[5], 71), 0)
    left_roots = draw_left_roots(jax.random.fold_in(splits[5], 71), 0)
    right_roots = draw_right_roots(jax.random.fold_in(splits[5], 71), 0)
    owners = draw_owners(jax.random.fold_in(splits[5], 71), 0)
    return dict(gradients=gradients, second_moment=second_moment, left_roots=left_roots, right_roots=right_roots, owners=owners)


moment_decay = 0.999
adam_eps = 1e-08
norm_eps = 1e-06
learn_rate = 0.05

def block_slots(owners):
    block_count = owners.shape[0]
    positions = jnp.arange(block_count, dtype=jnp.int32)
    same_owner = (owners[:, None] == owners[None, :]) & (positions[None, :] < positions[:, None])
    return lax.optimization_barrier(jnp.sum(same_owner.astype(jnp.int32), axis=1)).astype(jnp.int32)

def reference(gradients, second_moment, left_roots, right_roots, owners):
    summed = lax.optimization_barrier(jnp.sum(gradients.astype(jnp.float32), axis=0))
    moment = moment_decay * second_moment + (1.0 - moment_decay) * summed * summed
    adam_dir = summed / (jnp.sqrt(moment) + adam_eps)
    col_blocks = CW // BS
    squares = lax.optimization_barrier(jnp.sum((adam_dir * adam_dir).reshape(NBR, BS, col_blocks, BS), axis=(1, 3)))
    adam_norm = jnp.sqrt(squares.reshape(NBLK))
    slot_total = SLOT_REP * N_REP
    holder_pos = (owners * slot_total + block_slots(owners)).astype(jnp.int32)
    left_all = left_roots.reshape(N_FSDP * slot_total, BS, BS)
    right_all = right_roots.reshape(N_FSDP * slot_total, BS, BS)
    blocks = summed.reshape(NBR, BS, col_blocks, BS).transpose(0, 2, 1, 3).reshape(NBLK, BS, BS)

    def single(packed):
        grad_block, position, target = packed
        left_factor = left_all[position]
        right_factor = right_all[position]
        half_way = jnp.dot(left_factor, grad_block, precision=lax.Precision.HIGHEST, preferred_element_type=jnp.float32)
        precond = jnp.dot(half_way, right_factor, precision=lax.Precision.HIGHEST, preferred_element_type=jnp.float32)
        graft_ratio = target / (jnp.sqrt(jnp.sum(precond * precond)) + norm_eps)
        return (-learn_rate * precond * graft_ratio).astype(jnp.bfloat16)
    result = lax.map(single, (blocks, holder_pos, adam_norm))
    return result.reshape(NBR, col_blocks, BS, BS).transpose(0, 2, 1, 3).reshape(NBR, BS, CW)
```

```python
import functools
import jax
import jax.numpy as jnp
from jax import lax
from jax.experimental import pallas as pl
from jax.experimental.pallas import tpu as pltpu
from jax.sharding import PartitionSpec as P

moment_decay = 0.999
adam_eps = 1e-08
norm_eps = 1e-06
learn_rate = 0.05

BF = jnp.bfloat16
F32 = jnp.float32
MESH = pl.DeviceIdType.MESH
N_FSDP = 64
N_REP = 4
SLOTS = 3
NBLK = 320
COLB = 40
QCOL = 10
STRIP = (32, 128)
LIST = 240
CHUNKS = ((0, 32), (32, 32), (64, 32), (96, 32), (128, 32), (160, 40), (200, 40))
OUT_LIST = 160
OUT_AT = {1: 0, 0: 64, 2: 128}
OUT_LEN = {1: 64, 0: 64, 2: 32}
VMEM_LIMIT = 56 << 20


def owner_at(half, k):
    z = k // 4
    y = 2 * ((k // 2) % 2) + (z + half) % 2
    return z * 8 + y * 2 + k % 2


def split(x):
    hi = x.astype(BF)
    return hi, (x - hi.astype(F32)).astype(BF)


def mm(a, b):
    return jnp.dot(a, b, preferred_element_type=F32)


def exchange(ids, rank, slot2, grads, second, left, right, ag, sq,
             sa, ra, sb, rb, rb2, outgoing, arriving, g32, gbf, lbuf, rbuf, lhi, llo, rhi, rlo,
             pm, ps, u2, p2, acc, t1, t2, t3, n1, n2, n3,
             x_send, x_recv, a_send, a_recv, o_send, o_recv, g_send, g_recv, n_send, n_recv, loc):
    f = lax.axis_index("fsdp")
    r = lax.axis_index("rep")
    rt, lt, opp = (r + 1) % 4, (r + 3) % 4, (r + 2) % 4
    z, yc = f // 8, f % 8

    factor_copies = [pltpu.make_async_copy(left, lbuf, loc.at[0]), pltpu.make_async_copy(right, rbuf, loc.at[1])]
    for cp in factor_copies:
        cp.start()

    barrier = pltpu.get_barrier_semaphore()

    def greet(k, carry):
        pl.semaphore_signal(barrier, inc=1, device_id=((f + k) % N_FSDP, r), device_id_type=MESH)
        return carry

    lax.fori_loop(1, N_FSDP, greet, 0)
    for other in (rt, lt, opp):
        pl.semaphore_signal(barrier, inc=1, device_id=(f, other), device_id_type=MESH)

    def own(target, e):
        return grads[ids[target * LIST + e]]

    def own32(target, e):
        return own(target, e).astype(F32)

    def x_copy(c, kind, src, dst, to):
        return pltpu.make_async_remote_copy(src_ref=src, dst_ref=dst, send_sem=x_send.at[c, kind],
                                            recv_sem=x_recv.at[c, kind], device_id=(f, to), device_id_type=MESH)

    def rb_at(c, side, a, n):
        return rb2.at[side, pl.ds(a, n)] if c == 0 else rb.at[side, pl.ds(a, n)]

    def x_copies(c, kinds):
        lo, n = CHUNKS[c]
        h = n // 2
        every = (
            lambda: x_copy(c, 0, sa.at[pl.ds(lo, h)], ra.at[pl.ds(lo, h)], rt),
            lambda: x_copy(c, 1, sa.at[pl.ds(lo + h, h)], ra.at[pl.ds(lo + h, h)], lt),
            lambda: x_copy(c, 2, sb.at[0, pl.ds(lo + h, h)], rb_at(c, 0, lo + h, h), rt),
            lambda: x_copy(c, 3, sb.at[1, pl.ds(lo, h)], rb_at(c, 1, lo, h), lt),
            lambda: x_copy(c, 4, sb.at[0, pl.ds(lo, h)], rb_at(c, 0, lo, h), rt),
            lambda: x_copy(c, 5, sb.at[1, pl.ds(lo + h, h)], rb_at(c, 1, lo + h, h), lt),
        )
        return [every[k]() for k in kinds]

    def fill_a(c):
        lo, n = CHUNKS[c]
        h = n // 2

        def body(k, carry):
            sa[lo + k] = own(opp, lo + k)
            sa[lo + h + k] = own(opp, lo + h + k)
            sb[0, lo + h + k] = own(rt, lo + h + k)
            sb[1, lo + k] = own(lt, lo + k)
            return carry

        lax.fori_loop(0, h, body, 0, unroll=4)

    def step_a(c):
        fill_a(c)
        for cp in x_copies(c, (0, 1, 2, 3)):
            cp.start()

    def step_b(c):
        lo, n = CHUNKS[c]
        h = n // 2
        for cp in x_copies(c, (0, 1)):
            cp.wait_recv()

        def body(k, carry):
            e, g = lo + k, lo + h + k
            sb[0, e] = (own32(rt, e) + ra[e].astype(F32)).astype(BF)
            sb[1, g] = (own32(lt, g) + ra[g].astype(F32)).astype(BF)
            return carry

        lax.fori_loop(0, h, body, 0, unroll=4)
        for cp in x_copies(c, (4, 5)):
            cp.start()

    def wait_b(c):
        for cp in x_copies(c, (2, 3, 4, 5)):
            cp.wait_recv()

    def a_copy(s, d, k):
        return pltpu.make_async_remote_copy(src_ref=outgoing.at[s, d], dst_ref=arriving.at[s, f],
                                            send_sem=a_send.at[s, d], recv_sem=a_recv.at[s, f],
                                            device_id=(d, r), device_id_type=MESH)

    def a_go(s, d):
        @pl.when(d != f)
        def _():
            a_copy(s, d, 0).start()

        @pl.when(d == f)
        def _():
            arriving[s, f] = outgoing[s, d]

    def step_f(c):
        wait_b(c)
        if c == 0:
            def body(d, carry):
                p = rank[r * N_FSDP + d]
                total = own32(r, p) + rb2[0, p].astype(F32) + rb2[1, p].astype(F32)
                outgoing[2, d] = total.astype(BF)
                return carry

            lax.fori_loop(0, N_FSDP, body, 0, unroll=4)

            def go(k, carry):
                a_go(2, (f + k) % N_FSDP)
                return carry

            lax.fori_loop(0, N_FSDP, go, 0)
            return
        lo, n = CHUNKS[c]
        s, half = (c - 1) // 2, (c - 1) % 2

        def body(k, carry):
            e = lo + k
            total = own32(r, e) + rb[0, e].astype(F32) + rb[1, e].astype(F32)
            outgoing[s, owner_at(half, k)] = total.astype(BF)
            return carry

        lax.fori_loop(0, n, body, 0, unroll=4)

        def go(k, carry):
            a_go(s, owner_at(half, (z * 4 + k) % 32))
            return carry

        lax.fori_loop(0, n, go, 0)

    def prep(s):
        def body(k, carry):
            rows = pl.ds(pl.multiple_of(k * 64, 64), 64)
            lhi[s, rows, :], llo[s, rows, :] = split(lbuf[s, rows, :])
            rhi[s, rows, :], rlo[s, rows, :] = split(rbuf[s, rows, :])
            return carry

        lax.fori_loop(0, 8, body, 0)

    def product(s):
        def arrived(k, carry):
            src = (f + k) % N_FSDP
            pltpu.make_async_remote_copy(src_ref=outgoing.at[s, src], dst_ref=arriving.at[s, src],
                                         send_sem=a_send.at[s, src], recv_sem=a_recv.at[s, src],
                                         device_id=(src, r), device_id_type=MESH).wait_recv()
            return carry

        lax.fori_loop(1, N_FSDP, arrived, 0)

        def gather(m, carry):
            x = arriving[s, m].astype(F32)
            for t in range(4):
                g32[pl.ds(pl.multiple_of(m * 8, 8), 8), t * 128:(t + 1) * 128] = x[t * 8:(t + 1) * 8]
            return carry

        lax.fori_loop(0, N_FSDP, gather, 0, unroll=4)
        gbf[...] = g32[...].astype(BF)

        def rows_of(k, total):
            rows = pl.ds(pl.multiple_of(k * 128, 128), 128)
            half_way = mm(lhi[s, rows, :], gbf[...]) + mm(llo[s, rows, :], gbf[...])
            hhi, hlo = split(half_way)
            p = mm(hhi, rhi[s]) + (mm(hlo, rhi[s]) + mm(hhi, rlo[s]))
            pm[rows, :] = p
            q = p * p
            q = q.reshape(16, 8, 512).sum(axis=0)
            return total + (q[:, 0:128] + q[:, 128:256] + q[:, 256:384] + q[:, 384:512])

        total = lax.fori_loop(0, 4, rows_of, jnp.zeros((8, 128), F32))
        total = jnp.sum(jnp.sum(total, axis=0, keepdims=True), axis=1, keepdims=True)
        scale = -learn_rate / (jnp.sqrt(total) + norm_eps)

        def cut(m, carry):
            y = pm[pl.ds(pl.multiple_of(m * 8, 8), 8), :] * scale
            y = jnp.concatenate([y[:, t * 128:(t + 1) * 128] for t in range(4)], axis=0)
            ps[s, m] = y.astype(BF)
            return carry

        lax.fori_loop(0, N_FSDP, cut, 0, unroll=4)

    def o_copy(s, d, src):
        dst = u2.at[src] if s == 2 else ag.at[r, OUT_AT[s] + src]
        return pltpu.make_async_remote_copy(src_ref=ps.at[s, d], dst_ref=dst, send_sem=o_send.at[s, d],
                                            recv_sem=o_recv.at[s, src], device_id=(d, r), device_id_type=MESH)

    def o_self(s):
        dst = u2.at[f] if s == 2 else ag.at[r, OUT_AT[s] + f]
        return pltpu.make_async_copy(ps.at[s, f], dst, loc.at[2 + s])

    def send_out(s):
        o_self(s).start()

        def go(k, carry):
            o_copy(s, (f + k) % N_FSDP, f).start()
            return carry

        lax.fori_loop(1, N_FSDP, go, 0)

    def wait_out(s):
        o_self(s).wait()

        def arrived(k, carry):
            src = (f + k) % N_FSDP
            o_copy(s, src, src).wait_recv()
            return carry

        lax.fori_loop(1, N_FSDP, arrived, 0)

    def g_copy(s, kind, rep, a, n, to, src=None):
        here = ag.at[rep, pl.ds(OUT_AT[s] + a, n)]
        return pltpu.make_async_remote_copy(src_ref=here if src is None else src, dst_ref=here,
                                            send_sem=g_send.at[s, kind], recv_sem=g_recv.at[s, kind],
                                            device_id=(f, to), device_id_type=MESH)

    def g_copies(s, kinds):
        n = OUT_LEN[s]
        h = n // 2
        src = p2 if s == 2 else None
        every = (
            lambda: g_copy(s, 0, r, 0, n, rt, src),
            lambda: g_copy(s, 1, r, 0, n, lt, src),
            lambda: g_copy(s, 2, lt, 0, h, rt),
            lambda: g_copy(s, 3, rt, h, h, lt),
        )
        return [every[k]() for k in kinds]

    def own_two():
        return pltpu.make_async_copy(p2, ag.at[r, pl.ds(OUT_AT[2], OUT_LEN[2])], loc.at[5])

    def gather_one(s):
        wait_out(s)
        if s == 2:
            def body(p, carry):
                p2[p] = u2[slot2[r * 32 + p]]
                return carry

            lax.fori_loop(0, 32, body, 0, unroll=4)
            own_two().start()
        for cp in g_copies(s, (0, 1)):
            cp.start()

    def gather_two(s):
        for k in (0, 1):
            g_copies(s, (k,))[0].wait_recv()
            g_copies(s, (k + 2,))[0].start()

    def gather_end(s):
        for cp in g_copies(s, (2, 3)):
            cp.wait_recv()

    def adam():
        wait_b(5)
        wait_b(6)

        def body(k, carry):
            e = 160 + k
            total = own32(r, e) + rb[0, e].astype(F32) + rb[1, e].astype(F32)
            moment = moment_decay * second[k] + (1.0 - moment_decay) * total * total
            step = total / (jnp.sqrt(moment) + adam_eps)
            sums = jnp.sum(step * step, axis=0, keepdims=True)
            acc[pl.ds(k, 1), :] = sums
            return carry

        acc[pl.ds(80, 48), :] = jnp.zeros((48, 128), F32)
        lax.fori_loop(0, 80, body, 0, unroll=2)
        ones = jnp.ones((8, 128), F32)
        t1[...] = lax.dot_general(ones, acc[...], (((1,), (1,)), ((), ())),
                                  precision=lax.Precision.HIGHEST, preferred_element_type=F32)

    def n_copy(stage, k):
        if stage == 0:
            src, dst, to, at = t1, n1.at[yc], (z * 8 + (yc + k) % 8, r), k
        elif stage == 1:
            src, dst, to, at = t2, n2.at[z], (((z + k) % 8) * 8 + yc, r), 8 + k
        else:
            src, dst, to, at = t3, n3.at[r], (f, (r + k) % 4), 16 + k
        return pltpu.make_async_remote_copy(src_ref=src, dst_ref=dst, send_sem=n_send.at[at],
                                            recv_sem=n_recv.at[at], device_id=to, device_id_type=MESH)

    def n_start(stage):
        for k in range(1, 4 if stage == 2 else 8):
            n_copy(stage, k).start()

    def n_sum(stage):
        me, own_tile, got, out = ((yc, t1, n1, t2), (z, t2, n2, t3))[stage]
        got[me] = own_tile[...]
        for k in range(1, 8):
            n_copy(stage, k).wait_recv()
        out[...] = jnp.sum(got[...], axis=0)

    def n_end():
        n3[r] = t3[...]
        for k in range(1, 4):
            n_copy(2, k).wait_recv()
        sq[...] = n3[...]

    fill_a(0)
    pl.semaphore_wait(barrier, N_FSDP - 1 + 3)
    for cp in x_copies(0, (0, 1, 2, 3)):
        cp.start()
    step_a(1)
    step_b(0)
    step_a(2)
    step_f(0)
    step_b(1)
    step_a(3)
    step_f(1)
    step_b(2)
    step_a(4)
    for cp in factor_copies:
        cp.wait()
    step_f(2)
    step_b(3)
    prep(2)
    step_f(3)
    step_b(4)
    step_a(5)
    step_a(6)
    prep(0)
    prep(1)
    step_f(4)
    step_b(5)
    product(2)
    send_out(2)
    step_b(6)
    product(0)
    send_out(0)
    gather_one(2)
    product(1)
    send_out(1)
    adam()
    n_start(0)
    gather_two(2)
    n_sum(0)
    n_start(1)
    gather_one(0)
    gather_two(0)
    n_sum(1)
    n_start(2)
    gather_one(1)
    gather_two(1)
    n_end()
    own_two().wait()
    for s in (2, 0, 1):
        gather_end(s)

    for c in range(len(CHUNKS)):
        for cp in x_copies(c, range(6)):
            cp.wait_send()
    for s in range(SLOTS):
        def sent(k, carry, s=s):
            d = (f + k) % N_FSDP
            a_copy(s, d, k).wait_send()
            o_copy(s, d, f).wait_send()
            return carry

        lax.fori_loop(1, N_FSDP, sent, 0)
        for cp in g_copies(s, range(4)):
            cp.wait_send()
    for stage in range(3):
        for k in range(1, 4 if stage == 2 else 8):
            n_copy(stage, k).wait_send()


def place(pos, ag, sq, out, norm):
    ones = jnp.where(lax.broadcasted_iota(jnp.int32, (8, 128), 0) == 0, 1.0, 0.0).astype(F32)
    for q in range(N_REP):
        rows = lax.dot_general(sq[q], ones, (((0,), (0,)), ((), ())),
                               precision=lax.Precision.HIGHEST, preferred_element_type=F32)
        norm[q * 128:(q + 1) * 128, :] = jnp.sqrt(rows)

    def line(i, carry):
        for q in range(N_REP):
            for j in range(QCOL):
                b = i * COLB + q * QCOL + j
                scale = norm[pl.ds(q * 128 + i * QCOL + j, 1), :]
                out[b] = (ag[pos[b]].astype(F32) * scale).astype(BF)
        return carry

    lax.fori_loop(0, NBLK // COLB, line, 0)


def tables(owners):
    blocks = jnp.arange(NBLK, dtype=jnp.int32)
    earlier = (owners[:, None] == owners[None, :]) & (blocks[None, :] < blocks[:, None])
    slot = jnp.sum(earlier.astype(jnp.int32), axis=1)
    s, rep = slot // N_REP, slot % N_REP
    key = (s * N_REP + rep) * N_FSDP + owners
    places = jnp.arange(SLOTS * N_REP * N_FSDP, dtype=jnp.int32)
    holder = jnp.sum(jnp.where(key[None, :] == places[:, None], blocks[None, :] + 1, 0), axis=1) - 1
    holder = holder.reshape(SLOTS, N_REP, N_FSDP)
    filled = holder[2] >= 0
    people = jnp.arange(N_FSDP, dtype=jnp.int32)
    rank = jnp.sum((filled[:, None, :] & (people[None, None, :] < people[None, :, None])).astype(jnp.int32), axis=2)
    rank = jnp.minimum(rank, 31)
    at = (rank[:, :, None] == jnp.arange(32, dtype=jnp.int32)[None, None, :]) & filled[:, :, None]
    packed = jnp.sum(jnp.where(at, holder[2][:, :, None], 0), axis=1)
    slot2 = jnp.sum(jnp.where(at, people[None, :, None], 0), axis=1)
    order = [owner_at(half, k) for half in range(2) for k in range(32)]
    order = jnp.asarray(order, jnp.int32)
    safe = jnp.maximum(holder, 0)
    k = jnp.arange(80, dtype=jnp.int32)
    quarter = (k // QCOL) * COLB + k % QCOL
    quarter = quarter[None, :] + QCOL * jnp.arange(N_REP, dtype=jnp.int32)[:, None]
    ids = jnp.concatenate([packed, safe[0][:, order], safe[1][:, order], quarter], axis=1)
    rank_of = jnp.sum(jnp.where(rep[:, None] == jnp.arange(N_REP)[None, :], rank[:, owners].T, 0), axis=1)
    entry = jnp.where(s == 1, OUT_AT[1] + owners, jnp.where(s == 0, OUT_AT[0] + owners, OUT_AT[2] + rank_of))
    pos = rep * OUT_LIST + entry
    return ids.reshape(-1), rank.reshape(-1), slot2.reshape(-1), pos


def shards(gradients, second_moment, left_roots, right_roots, owners):
    ids, rank, slot2, pos = tables(owners)
    grads = gradients.reshape(8, 8, 160, 128).transpose(0, 2, 1, 3).reshape(NBLK, *STRIP)
    second = second_moment.reshape(8, 8, 40, 128).transpose(0, 2, 1, 3).reshape(80, *STRIP)
    left = left_roots.reshape(SLOTS, 512, 512)
    right = right_roots.reshape(SLOTS, 512, 512)
    smem = pl.BlockSpec(memory_space=pltpu.SMEM)
    vmem = pl.BlockSpec(memory_space=pltpu.VMEM)
    hbm = pl.BlockSpec(memory_space=pl.ANY)
    dma = pltpu.SemaphoreType.DMA
    vm = pltpu.VMEM
    chunks = len(CHUNKS)
    ag, sq = pl.pallas_call(
        exchange,
        out_shape=(
            jax.ShapeDtypeStruct((N_REP, OUT_LIST, *STRIP), BF),
            jax.ShapeDtypeStruct((N_REP, 8, 128), F32),
        ),
        in_specs=[smem, smem, smem, vmem, vmem, hbm, hbm],
        out_specs=(hbm, vmem),
        scratch_shapes=[
            vm((LIST, *STRIP), BF), vm((LIST, *STRIP), BF),
            vm((2, LIST, *STRIP), BF), vm((2, LIST, *STRIP), BF), vm((2, 32, *STRIP), BF),
            vm((SLOTS, N_FSDP, *STRIP), BF), vm((SLOTS, N_FSDP, *STRIP), BF),
            vm((512, 512), F32), vm((512, 512), BF),
            vm((SLOTS, 512, 512), F32), vm((SLOTS, 512, 512), F32),
            vm((SLOTS, 512, 512), BF), vm((SLOTS, 512, 512), BF),
            vm((SLOTS, 512, 512), BF), vm((SLOTS, 512, 512), BF),
            vm((512, 512), F32), vm((SLOTS, N_FSDP, *STRIP), BF),
            vm((N_FSDP, *STRIP), BF), vm((32, *STRIP), BF), vm((128, 128), F32),
            vm((8, 128), F32), vm((8, 128), F32), vm((8, 128), F32),
            vm((8, 8, 128), F32), vm((8, 8, 128), F32), vm((N_REP, 8, 128), F32),
            dma((chunks, 6)), dma((chunks, 6)),
            dma((SLOTS, N_FSDP)), dma((SLOTS, N_FSDP)),
            dma((SLOTS, N_FSDP)), dma((SLOTS, N_FSDP)),
            dma((SLOTS, 4)), dma((SLOTS, 4)),
            dma((20,)), dma((20,)), dma((6,)),
        ],
        compiler_params=pltpu.CompilerParams(collective_id=0, has_side_effects=True, vmem_limit_bytes=VMEM_LIMIT),
        name="exchange",
    )(ids, rank, slot2, grads, second, left, right)
    out = pl.pallas_call(
        place,
        out_shape=jax.ShapeDtypeStruct((NBLK, *STRIP), BF),
        in_specs=[smem, vmem, vmem],
        out_specs=vmem,
        scratch_shapes=[vm((N_REP * 128, 128), F32)],
        compiler_params=pltpu.CompilerParams(vmem_limit_bytes=VMEM_LIMIT),
        name="place",
    )(pos, ag.reshape(N_REP * OUT_LIST, *STRIP), sq)
    return out.reshape(8, 160, 8, 128).transpose(0, 2, 1, 3).reshape(8, 8, 20480)


def solution(mesh):
    return jax.shard_map(
        shards,
        mesh=mesh,
        in_specs=(
            P("rep", None, "fsdp", None),
            P(None, "fsdp", "rep"),
            P("fsdp", None, "rep", None, None),
            P("fsdp", None, "rep", None, None),
            P(),
        ),
        out_specs=P(None, "fsdp", None),
        check_vma=False,
    )
```

```python
import functools
import jax
import jax.numpy as jnp
from jax import lax
from jax.experimental import pallas as pl
from jax.experimental.pallas import tpu as pltpu
from jax.sharding import PartitionSpec as P

moment_decay = 0.999
adam_eps = 1e-08
norm_eps = 1e-06
learn_rate = 0.05

BF = jnp.bfloat16
F32 = jnp.float32
MESH = pl.DeviceIdType.MESH
N_FSDP = 64
N_REP = 4
NBLK = 320
SLOTS = 3
COLB = 40
QCOL = 10
HALF = (16, 128)
PACKED = 64
LIST = 208
CHUNKS = ((0, 64, 0, 0), (64, 64, 0, 1), (128, 64, 64, 0), (192, 64, 64, 1), (256, 80, 128, 0), (336, 80, 128, 1))
ENTRIES = 416
PARTS = 4
RANK, WHO, POS = 4, 6, 7
VMEM_LIMIT = 56 << 20


def split(x):
    hi = x.astype(BF)
    return hi, (x - hi.astype(F32)).astype(BF)


def mm(a, b):
    return jnp.dot(a, b, preferred_element_type=F32)


def exchange(tab, grads, second, left, right, ag, sq,
             sa, ra, sb, rb, rbp0, rbp1, outgoing, arriving, g32, gbf, lbuf, rbuf, lhi, llo, rhi, rlo, vbuf,
             pm, ps, u0, u1, pk, acc, t1, t2, t3, n1, n2, n3,
             x_send, x_recv, a_send, a_recv, o_send, o_recv, g_send, g_recv, n_send, n_recv, loc):
    f = lax.axis_index("fsdp")
    r = lax.axis_index("rep")
    rt, lt, opp = (r + 1) % 4, (r + 3) % 4, (r + 2) % 4
    z, yc = f // 8, f % 8
    peer = ((f + 1) % N_FSDP, r)
    rbp, u = (rbp0, rbp1), (u0, u1)

    barrier = pltpu.get_barrier_semaphore()
    for other in (rt, lt, opp):
        pl.semaphore_signal(barrier, inc=1, device_id=(f, other), device_id_type=MESH)

    def greet(k, carry):
        pl.semaphore_signal(barrier, inc=1, device_id=((f + k) % N_FSDP, r), device_id_type=MESH)
        return carry

    lax.fori_loop(1, N_FSDP, greet, 0)

    loads = [pltpu.make_async_copy(left, lbuf, loc.at[0]), pltpu.make_async_copy(right, rbuf, loc.at[1]),
             pltpu.make_async_copy(second, vbuf, loc.at[2])]
    for cp in loads:
        cp.start()

    def own(c, target, k):
        return grads[tab[target, CHUNKS[c][2] + k], CHUNKS[c][3]]

    def own32(c, target, k):
        return own(c, target, k).astype(F32)

    def remote(src, dst, send, recv, to):
        return pltpu.make_async_remote_copy(src_ref=src, dst_ref=dst, send_sem=send, recv_sem=recv,
                                            device_id=to, device_id_type=MESH)

    def rb_at(c, side, k, n):
        return rbp[c].at[side, pl.ds(k, n)] if c < 2 else rb.at[side, pl.ds(CHUNKS[c][0] + k, n)]

    def x_copies(c, kinds):
        lo, n = CHUNKS[c][:2]
        h = n // 2
        first, last = pl.ds(lo, h), pl.ds(lo + h, h)
        right_to, left_to = (f, rt), (f, lt)
        one, two = x_recv.at[c, 0], x_recv.at[c, 1]
        every = (
            lambda: remote(sa.at[first], ra.at[first], x_send.at[0], one, right_to),
            lambda: remote(sa.at[last], ra.at[last], x_send.at[0], one, left_to),
            lambda: remote(sb.at[0, last], rb_at(c, 0, h, h), x_send.at[1], two, right_to),
            lambda: remote(sb.at[1, first], rb_at(c, 1, 0, h), x_send.at[2], two, left_to),
            lambda: remote(sb.at[0, first], rb_at(c, 0, 0, h), x_send.at[1], two, right_to),
            lambda: remote(sb.at[1, last], rb_at(c, 1, h, h), x_send.at[2], two, left_to),
        )
        return [every[k]() for k in kinds]

    def fill_a(c):
        lo, n = CHUNKS[c][:2]
        h = n // 2

        def body(k, carry):
            sa[lo + k] = own(c, opp, k)
            sa[lo + h + k] = own(c, opp, h + k)
            sb[0, lo + h + k] = own(c, rt, h + k)
            sb[1, lo + k] = own(c, lt, k)
            return carry

        lax.fori_loop(0, h, body, 0, unroll=4)

    def send_a(c):
        for cp in x_copies(c, (0, 1, 2, 3)):
            cp.start()

    def step_a(c):
        fill_a(c)
        send_a(c)

    def step_b(c):
        lo, n = CHUNKS[c][:2]
        h = n // 2
        both = pl.ds(lo, n)
        remote(sa.at[both], ra.at[both], x_send.at[0], x_recv.at[c, 0], (f, rt)).wait_recv()

        def body(k, carry):
            e, g = lo + k, lo + h + k
            sb[0, e] = (own32(c, rt, k) + ra[e].astype(F32)).astype(BF)
            sb[1, g] = (own32(c, lt, h + k) + ra[g].astype(F32)).astype(BF)
            return carry

        lax.fori_loop(0, h, body, 0, unroll=4)
        for cp in x_copies(c, (4, 5)):
            cp.start()

    def wait_b(c):
        lo, n = CHUNKS[c][:2]
        both = sb.at[:, pl.ds(lo, n)]
        remote(both, both, x_send.at[1], x_recv.at[c, 1], (f, rt)).wait_recv()

    def most(s, half, buf, send, recv):
        part = buf.at[s, half, pl.ds(0, N_FSDP - 1)]
        return remote(part, part, send.at[s, half], recv.at[s, half], peer)

    def to_owners(s, half, total):
        def body(k, carry):
            d = (f + k) % N_FSDP
            outgoing[s, half, d] = total(d).astype(BF)
            remote(outgoing.at[s, half, d], arriving.at[s, half, f], a_send.at[s, half], a_recv.at[s, half],
                   (d, r)).start()
            return carry

        lax.fori_loop(1, N_FSDP, body, 0, unroll=3)
        arriving[s, half, f] = total(f).astype(BF)

    def step_f(half):
        c = 2 + half
        lo = CHUNKS[c][0]
        wait_b(c)
        to_owners(0, half, lambda d: own32(c, r, d) + rb[0, lo + d].astype(F32) + rb[1, lo + d].astype(F32))

    def step_p(half):
        got = rbp[half]
        wait_b(half)
        for s in (1, 2):
            def total(d, s=s):
                p = tab[RANK + s - 1, r * N_FSDP + d]
                return own32(half, r, p) + got[0, p].astype(F32) + got[1, p].astype(F32)

            to_owners(s, half, total)

    def prep(s):
        def body(k, carry):
            rows = pl.ds(pl.multiple_of(k * 64, 64), 64)
            lhi[s, rows, :], llo[s, rows, :] = split(lbuf[s, rows, :])
            rhi[s, rows, :], rlo[s, rows, :] = split(rbuf[s, rows, :])
            return carry

        lax.fori_loop(0, 8, body, 0)

    def product(s):
        for half in range(2):
            most(s, half, arriving, a_send, a_recv).wait_recv()

            def gather(m, carry, half=half):
                x = arriving[s, half, m].astype(F32)
                for t in range(2):
                    cols = slice(half * 256 + t * 128, half * 256 + (t + 1) * 128)
                    g32[pl.ds(pl.multiple_of(m * 8, 8), 8), cols] = x[t * 8:(t + 1) * 8]
                return carry

            lax.fori_loop(0, N_FSDP, gather, 0, unroll=4)
        gbf[...] = g32[...].astype(BF)

        def rows_of(k, total):
            rows = pl.ds(pl.multiple_of(k * 128, 128), 128)
            half_way = mm(lhi[s, rows, :], gbf[...]) + mm(llo[s, rows, :], gbf[...])
            hhi, hlo = split(half_way)
            p = mm(hhi, rhi[s]) + (mm(hlo, rhi[s]) + mm(hhi, rlo[s]))
            pm[s, rows, :] = p
            q = p * p
            q = q.reshape(16, 8, 512).sum(axis=0)
            return total + (q[:, 0:128] + q[:, 128:256] + q[:, 256:384] + q[:, 384:512])

        total = lax.fori_loop(0, 4, rows_of, jnp.zeros((8, 128), F32))
        total = jnp.sum(jnp.sum(total, axis=0, keepdims=True), axis=1, keepdims=True)
        return -learn_rate / (jnp.sqrt(total) + norm_eps)

    def landing(s, half, src):
        return ag.at[r, half, src] if s == 0 else u[half].at[s - 1, src]

    def o_self(s, half):
        return pltpu.make_async_copy(ps.at[s, half, f], landing(s, half, f), loc.at[3 + s * 2 + half])

    def send_out(s, half, scale):
        def cut(d):
            y = pm[s, pl.ds(pl.multiple_of(d * 8, 8), 8), half * 256:(half + 1) * 256] * scale
            ps[s, half, d] = jnp.concatenate([y[:, 0:128], y[:, 128:256]], axis=0).astype(BF)

        def go(k, carry):
            d = (f + k) % N_FSDP
            cut(d)
            remote(ps.at[s, half, d], landing(s, half, f), o_send.at[s, half], o_recv.at[s, half], (d, r)).start()
            return carry

        lax.fori_loop(1, N_FSDP, go, 0, unroll=3)
        cut(f)
        o_self(s, half).start()

    def wait_out(s, half):
        o_self(s, half).wait()
        most(s, half, ps, o_send, o_recv).wait_recv()

    def g_copy(part, kind, rep, a, n, to):
        here = ag.at[rep, part, pl.ds(a, n)]
        src = pk.at[part - 2] if part >= 2 and kind < 2 else here
        return remote(src, here, g_send.at[part], g_recv.at[part, min(kind, 2)], (f, to))

    def g_copies(part, kinds):
        every = (
            lambda: g_copy(part, 0, r, 0, 64, rt),
            lambda: g_copy(part, 1, r, 0, 64, lt),
            lambda: g_copy(part, 2, lt, 0, 32, rt),
            lambda: g_copy(part, 3, rt, 32, 32, lt),
        )
        return [every[k]() for k in kinds]

    def own_packed(half):
        return pltpu.make_async_copy(pk.at[half], ag.at[r, 2 + half], loc.at[9 + half])

    def gather_one(part):
        half = part % 2
        if part < 2:
            wait_out(0, half)
        else:
            wait_out(1, half)
            wait_out(2, half)

            def body(p, carry):
                pk[half, p] = u[half].reshape(128, *HALF)[tab[WHO, r * PACKED + p]]
                return carry

            lax.fori_loop(0, PACKED, body, 0, unroll=4)
            own_packed(half).start()
        for cp in g_copies(part, (0, 1)):
            cp.start()

    def gather_two(part):
        for k in (0, 1):
            g_copies(part, (k,))[0].wait_recv()
            g_copies(part, (k + 2,))[0].start()

    def gather_end(part):
        g_copy(part, 2, opp, 0, 64, rt).wait_recv()

    def adam():
        wait_b(4)
        wait_b(5)

        def one(c, k):
            lo = CHUNKS[c][0]
            return own32(c, r, k) + rb[0, lo + k].astype(F32) + rb[1, lo + k].astype(F32)

        def body(k, carry):
            total = jnp.concatenate([one(4, k), one(5, k)], axis=0)
            moment = moment_decay * vbuf[k] + (1.0 - moment_decay) * total * total
            step = total / (jnp.sqrt(moment) + adam_eps)
            acc[pl.ds(k, 1), :] = jnp.sum(step * step, axis=0, keepdims=True)
            return carry

        acc[pl.ds(80, 48), :] = jnp.zeros((48, 128), F32)
        lax.fori_loop(0, 80, body, 0, unroll=2)
        ones = jnp.ones((8, 128), F32)
        t1[...] = lax.dot_general(ones, acc[...], (((1,), (1,)), ((), ())),
                                  precision=lax.Precision.HIGHEST, preferred_element_type=F32)

    def n_parts(stage):
        return ((yc, t1, n1, t2), (z, t2, n2, t3), (r, t3, n3, None))[stage]

    def n_start(stage):
        me, tile, got, _ = n_parts(stage)
        for k in range(1, 4 if stage == 2 else 8):
            to = ((z * 8 + (yc + k) % 8, r), (((z + k) % 8) * 8 + yc, r), (f, (r + k) % 4))[stage]
            remote(tile, got.at[me], n_send.at[stage], n_recv.at[stage], to).start()
        got[me] = tile[...]

    def n_all(stage):
        got = n_parts(stage)[2]
        part = got.at[pl.ds(0, 3 if stage == 2 else 7)]
        return remote(part, part, n_send.at[stage], n_recv.at[stage], peer)

    def n_sum(stage):
        n_all(stage).wait_recv()
        _, _, got, out = n_parts(stage)
        if stage == 2:
            sq[...] = got[...]
        else:
            out[...] = jnp.sum(got[...], axis=0)

    fill_a(0)
    fill_a(1)
    pl.semaphore_wait(barrier, N_FSDP - 1 + 3)
    send_a(0)
    send_a(1)
    step_b(0)
    step_a(2)
    step_b(1)
    step_p(0)
    step_a(3)
    step_b(2)
    step_p(1)
    for cp in loads:
        cp.wait()
    prep(1)
    step_b(3)
    step_f(0)
    step_a(4)
    prep(2)
    scale1 = product(1)
    send_out(1, 0, scale1)
    step_f(1)
    scale2 = product(2)
    send_out(2, 0, scale2)
    send_out(1, 1, scale1)
    send_out(2, 1, scale2)
    step_b(4)
    step_a(5)
    prep(0)
    scale0 = product(0)
    send_out(0, 0, scale0)
    send_out(0, 1, scale0)
    step_b(5)
    gather_one(2)
    gather_one(3)
    gather_two(2)
    adam()
    n_start(0)
    gather_two(3)
    gather_one(0)
    n_sum(0)
    n_start(1)
    gather_two(0)
    gather_one(1)
    n_sum(1)
    n_start(2)
    gather_two(1)
    n_sum(2)
    for half in range(2):
        own_packed(half).wait()
    for part in (2, 3, 0, 1):
        gather_end(part)

    remote(sa, sa, x_send.at[0], x_recv.at[0, 0], (f, rt)).wait_send()
    for side in range(2):
        remote(sb.at[side], sb.at[side], x_send.at[1 + side], x_recv.at[0, 0], (f, rt)).wait_send()
    for s in range(SLOTS):
        for half in range(2):
            most(s, half, outgoing, a_send, a_recv).wait_send()
            most(s, half, ps, o_send, o_recv).wait_send()
    for part in range(PARTS):
        three = ag.at[pl.ds(0, 3), part]
        remote(three, three, g_send.at[part], g_recv.at[part, 0], (f, rt)).wait_send()
    for stage in range(3):
        n_all(stage).wait_send()


def place(tab, ag, sq, out, norm):
    ones = jnp.where(lax.broadcasted_iota(jnp.int32, (8, 128), 0) == 0, 1.0, 0.0).astype(F32)
    for q in range(N_REP):
        rows = lax.dot_general(sq[q], ones, (((0,), (0,)), ((), ())),
                               precision=lax.Precision.HIGHEST, preferred_element_type=F32)
        norm[q * 128:(q + 1) * 128, :] = jnp.sqrt(rows)

    def line(i, carry):
        for q in range(N_REP):
            for j in range(QCOL):
                b = i * COLB + q * QCOL + j
                scale = norm[pl.ds(q * 128 + i * QCOL + j, 1), :]
                p = tab[POS, b]
                for half in range(2):
                    out[b, half] = (ag[p + half * 64].astype(F32) * scale).astype(BF)
        return carry

    lax.fori_loop(0, NBLK // COLB, line, 0)


def tables(owners, tab):
    row = owners[...]
    sub = lax.broadcasted_iota(jnp.int32, (NBLK, NBLK), 0)
    lane = lax.broadcasted_iota(jnp.int32, (NBLK, NBLK), 1)

    def down(mask, value=1):
        return jnp.sum(jnp.where(mask, value, 0), axis=0, keepdims=True)

    def along(mask, value=1):
        return jnp.sum(jnp.where(mask, value, 0), axis=1, keepdims=True)

    col = along(sub == lane, row)
    same = col == row
    slot_c = along(same & (lane < sub))
    slot_r = down(same & (sub < lane))
    key_c, key_r = slot_c * N_FSDP + col, slot_r * N_FSDP + row
    alike = (slot_c & 3) == (slot_r & 3)
    rank_c = along(alike & (slot_r >= 4) & (key_r < key_c))
    rank_r = down(alike & (slot_c >= 4) & (key_c < key_r))
    code = jnp.where(slot_c < 4, key_c, 1024 + (slot_c & 3) * PACKED + rank_c)
    e = lax.broadcasted_iota(jnp.int32, (1, 256), 1)
    block = lax.broadcasted_iota(jnp.int32, (NBLK, 1), 0)
    a = e - 128
    line = sum(jnp.where(a >= QCOL * i, 1, 0) for i in range(1, 8))
    for t in range(N_REP):
        want = jnp.where(e < 64, 1024 + t * PACKED + e, t * N_FSDP + e - 64)
        found = down(code == want, block)
        mine = line * COLB + t * QCOL + a - line * QCOL
        tab[t:t + 1, 0:256] = jnp.where(e < 128, found, jnp.where(e < LIST, mine, 0))
    for s in (1, 2):
        tab[RANK + s - 1:RANK + s, 0:256] = down(key_c == s * 256 + e, rank_c)
    tab[WHO:WHO + 1, 0:256] = down(code == 1024 + e, ((slot_c >> 2) - 1) * N_FSDP + col)
    tab[POS:POS + 1, 0:NBLK] = (slot_r & 3) * 256 + jnp.where(slot_r < 4, row, 128 + rank_r)


def shards(gradients, second_moment, left_roots, right_roots, owners):
    grads = gradients.reshape(8, 8, 160, 128).transpose(0, 2, 1, 3).reshape(NBLK, 2, *HALF)
    second = second_moment.reshape(8, 8, 40, 128).transpose(0, 2, 1, 3).reshape(80, 32, 128)
    left = left_roots.reshape(SLOTS, 512, 512)
    right = right_roots.reshape(SLOTS, 512, 512)
    smem = pl.BlockSpec(memory_space=pltpu.SMEM)
    vmem = pl.BlockSpec(memory_space=pltpu.VMEM)
    hbm = pl.BlockSpec(memory_space=pl.ANY)
    dma = pltpu.SemaphoreType.DMA
    vm = pltpu.VMEM
    tab = pl.pallas_call(
        tables,
        out_shape=jax.ShapeDtypeStruct((8, 384), jnp.int32),
        in_specs=[vmem],
        out_specs=vmem,
        name="tables",
    )(owners.reshape(1, NBLK))
    ag, sq = pl.pallas_call(
        exchange,
        out_shape=(
            jax.ShapeDtypeStruct((N_REP, PARTS, 64, *HALF), BF),
            jax.ShapeDtypeStruct((N_REP, 8, 128), F32),
        ),
        in_specs=[smem, vmem, hbm, hbm, hbm],
        out_specs=(hbm, vmem),
        scratch_shapes=[
            vm((ENTRIES, *HALF), BF), vm((ENTRIES, *HALF), BF),
            vm((2, ENTRIES, *HALF), BF), vm((2, ENTRIES, *HALF), BF),
            vm((2, PACKED, *HALF), BF), vm((2, PACKED, *HALF), BF),
            vm((SLOTS, 2, N_FSDP, *HALF), BF), vm((SLOTS, 2, N_FSDP, *HALF), BF),
            vm((512, 512), F32), vm((512, 512), BF),
            vm((SLOTS, 512, 512), F32), vm((SLOTS, 512, 512), F32),
            vm((SLOTS, 512, 512), BF), vm((SLOTS, 512, 512), BF),
            vm((SLOTS, 512, 512), BF), vm((SLOTS, 512, 512), BF), vm((80, 32, 128), F32),
            vm((SLOTS, 512, 512), F32), vm((SLOTS, 2, N_FSDP, *HALF), BF),
            vm((2, N_FSDP, *HALF), BF), vm((2, N_FSDP, *HALF), BF), vm((2, PACKED, *HALF), BF), vm((128, 128), F32),
            vm((8, 128), F32), vm((8, 128), F32), vm((8, 128), F32),
            vm((8, 8, 128), F32), vm((8, 8, 128), F32), vm((N_REP, 8, 128), F32),
            dma((3,)), dma((len(CHUNKS), 2)),
            dma((SLOTS, 2)), dma((SLOTS, 2)), dma((SLOTS, 2)), dma((SLOTS, 2)),
            dma((PARTS,)), dma((PARTS, 3)), dma((3,)), dma((3,)), dma((11,)),
        ],
        compiler_params=pltpu.CompilerParams(collective_id=0, has_side_effects=True, vmem_limit_bytes=VMEM_LIMIT),
        name="exchange",
    )(tab, grads, second, left, right)
    out = pl.pallas_call(
        place,
        out_shape=jax.ShapeDtypeStruct((NBLK, 2, *HALF), BF),
        in_specs=[smem, vmem, vmem],
        out_specs=vmem,
        scratch_shapes=[vm((N_REP * 128, 128), F32)],
        compiler_params=pltpu.CompilerParams(vmem_limit_bytes=VMEM_LIMIT),
        name="place",
    )(tab, ag.reshape(N_REP * PARTS * 64, *HALF), sq)
    return out.reshape(8, 160, 8, 128).transpose(0, 2, 1, 3).reshape(8, 8, 20480)


def solution(mesh):
    return jax.shard_map(
        shards,
        mesh=mesh,
        in_specs=(
            P("rep", None, "fsdp", None),
            P(None, "fsdp", "rep"),
            P("fsdp", None, "rep", None, None),
            P("fsdp", None, "rep", None, None),
            P(),
        ),
        out_specs=P(None, "fsdp", None),
        check_vma=False,
    )
```

```python
import functools
import jax
import jax.numpy as jnp
from jax import lax
from jax.experimental import pallas as pl
from jax.experimental.pallas import tpu as pltpu
from jax.sharding import PartitionSpec as P

moment_decay = 0.999
adam_eps = 1e-08
norm_eps = 1e-06
learn_rate = 0.05

BF = jnp.bfloat16
F32 = jnp.float32
MESH = pl.DeviceIdType.MESH
N_FSDP = 64
N_REP = 4
NBLK = 320
SLOTS = 3
COLB = 40
QCOL = 10
HALF = (16, 128)
PACKED = 64
LIST = 208
CHUNKS = ((0, 64, 0, 0), (64, 64, 0, 1), (128, 64, 64, 0), (192, 64, 64, 1), (256, 80, 128, 0), (336, 80, 128, 1))
ENTRIES = 416
PARTS = 4
RANK, WHO, POS = 4, 6, 7
VMEM_LIMIT = 56 << 20


def split(x):
    hi = x.astype(BF)
    return hi, (x - hi.astype(F32)).astype(BF)


def mm(a, b):
    return jnp.dot(a, b, preferred_element_type=F32)


def exchange(tab, grads, second, left, right, ag, sq,
             sa, ra, sb, rb, rbp0, rbp1, outgoing, arriving, g32, gbf, lbuf, rbuf, lhi, llo, rhi, rlo, vbuf,
             pm, ps, u0, u1, pk, acc, t1, t2, t3, n1, n2, n3,
             x_send, x_recv, a_send, a_recv, o_send, o_recv, g_send, g_recv, n_send, n_recv, loc, lines):
    f = lax.axis_index("fsdp")
    r = lax.axis_index("rep")
    rt, lt, opp = (r + 1) % 4, (r + 3) % 4, (r + 2) % 4
    z, yc = f // 8, f % 8
    peer = ((f + 1) % N_FSDP, r)
    rbp, u = (rbp0, rbp1), (u0, u1)

    barrier = pltpu.get_barrier_semaphore()
    for other in (rt, lt, opp):
        pl.semaphore_signal(barrier, inc=1, device_id=(f, other), device_id_type=MESH)
    for k in range(1, 8):
        pl.semaphore_signal(barrier, inc=1, device_id=(z * 8 + (yc + k) % 8, r), device_id_type=MESH)
        pl.semaphore_signal(barrier, inc=1, device_id=(((z + k) % 8) * 8 + yc, r), device_id_type=MESH)

    loads = [pltpu.make_async_copy(left, lbuf, loc.at[0]), pltpu.make_async_copy(right, rbuf, loc.at[1]),
             pltpu.make_async_copy(second, vbuf, loc.at[2])]
    for cp in loads:
        cp.start()

    def own(c, target, k):
        return grads[tab[target, CHUNKS[c][2] + k], CHUNKS[c][3]]

    def own32(c, target, k):
        return own(c, target, k).astype(F32)

    def remote(src, dst, send, recv, to):
        return pltpu.make_async_remote_copy(src_ref=src, dst_ref=dst, send_sem=send, recv_sem=recv,
                                            device_id=to, device_id_type=MESH)

    def rb_at(c, side, k, n):
        return rbp[c].at[side, pl.ds(k, n)] if c < 2 else rb.at[side, pl.ds(CHUNKS[c][0] + k, n)]

    def x_copies(c, kinds):
        lo, n = CHUNKS[c][:2]
        h = n // 2
        first, last = pl.ds(lo, h), pl.ds(lo + h, h)
        right_to, left_to = (f, rt), (f, lt)
        one, two = x_recv.at[c, 0], x_recv.at[c, 1]
        every = (
            lambda: remote(sa.at[first], ra.at[first], x_send.at[0], one, right_to),
            lambda: remote(sa.at[last], ra.at[last], x_send.at[0], one, left_to),
            lambda: remote(sb.at[0, last], rb_at(c, 0, h, h), x_send.at[1], two, right_to),
            lambda: remote(sb.at[1, first], rb_at(c, 1, 0, h), x_send.at[2], two, left_to),
            lambda: remote(sb.at[0, first], rb_at(c, 0, 0, h), x_send.at[1], two, right_to),
            lambda: remote(sb.at[1, last], rb_at(c, 1, h, h), x_send.at[2], two, left_to),
        )
        return [every[k]() for k in kinds]

    def fill_a(c):
        lo, n = CHUNKS[c][:2]
        h = n // 2

        def body(k, carry):
            sa[lo + k] = own(c, opp, k)
            sa[lo + h + k] = own(c, opp, h + k)
            sb[0, lo + h + k] = own(c, rt, h + k)
            sb[1, lo + k] = own(c, lt, k)
            return carry

        lax.fori_loop(0, h, body, 0, unroll=4)

    def send_a(c):
        for cp in x_copies(c, (0, 1, 2, 3)):
            cp.start()

    def step_b(c):
        lo, n = CHUNKS[c][:2]
        h = n // 2
        both = pl.ds(lo, n)
        remote(sa.at[both], ra.at[both], x_send.at[0], x_recv.at[c, 0], (f, rt)).wait_recv()

        def body(k, carry):
            e, g = lo + k, lo + h + k
            sb[0, e] = (own32(c, rt, k) + ra[e].astype(F32)).astype(BF)
            sb[1, g] = (own32(c, lt, h + k) + ra[g].astype(F32)).astype(BF)
            return carry

        lax.fori_loop(0, h, body, 0, unroll=4)
        for cp in x_copies(c, (4, 5)):
            cp.start()

    def wait_b(c):
        lo, n = CHUNKS[c][:2]
        both = sb.at[:, pl.ds(lo, n)]
        remote(both, both, x_send.at[1], x_recv.at[c, 1], (f, rt)).wait_recv()

    def most(s, half, buf, send, recv):
        part = buf.at[s, half, pl.ds(0, N_FSDP - 1)]
        return remote(part, part, send.at[s, half], recv.at[s, half], peer)

    def to_owners(s, half, total):
        def body(k, carry):
            d = (f + k) % N_FSDP
            outgoing[s, half, d] = total(d).astype(BF)
            remote(outgoing.at[s, half, d], arriving.at[s, half, f], a_send.at[s, half], a_recv.at[s, half],
                   (d, r)).start()
            return carry

        lax.fori_loop(1, N_FSDP, body, 0, unroll=3)
        arriving[s, half, f] = total(f).astype(BF)

    def step_f(half):
        c = 2 + half
        lo = CHUNKS[c][0]
        wait_b(c)
        to_owners(0, half, lambda d: own32(c, r, d) + rb[0, lo + d].astype(F32) + rb[1, lo + d].astype(F32))

    def step_p(half):
        got = rbp[half]
        wait_b(half)
        for s in (1, 2):
            def total(d, s=s):
                p = tab[RANK + s - 1, r * N_FSDP + d]
                return own32(half, r, p) + got[0, p].astype(F32) + got[1, p].astype(F32)

            to_owners(s, half, total)

    def prep(s):
        def body(k, carry):
            rows = pl.ds(pl.multiple_of(k * 64, 64), 64)
            lhi[s, rows, :], llo[s, rows, :] = split(lbuf[s, rows, :])
            rhi[s, rows, :], rlo[s, rows, :] = split(rbuf[s, rows, :])
            return carry

        lax.fori_loop(0, 8, body, 0)

    def product(s):
        for half in range(2):
            most(s, half, arriving, a_send, a_recv).wait_recv()

            def gather(m, carry, half=half):
                x = arriving[s, half, m].astype(F32)
                for t in range(2):
                    cols = slice(half * 256 + t * 128, half * 256 + (t + 1) * 128)
                    g32[pl.ds(pl.multiple_of(m * 8, 8), 8), cols] = x[t * 8:(t + 1) * 8]
                return carry

            lax.fori_loop(0, N_FSDP, gather, 0, unroll=4)
        gbf[...] = g32[...].astype(BF)

        def rows_of(k, total):
            rows = pl.ds(pl.multiple_of(k * 128, 128), 128)
            half_way = mm(lhi[s, rows, :], gbf[...]) + mm(llo[s, rows, :], gbf[...])
            hhi, hlo = split(half_way)
            p = mm(hhi, rhi[s]) + (mm(hlo, rhi[s]) + mm(hhi, rlo[s]))
            pm[s, rows, :] = p
            q = p * p
            q = q.reshape(16, 8, 512).sum(axis=0)
            return total + (q[:, 0:128] + q[:, 128:256] + q[:, 256:384] + q[:, 384:512])

        total = lax.fori_loop(0, 4, rows_of, jnp.zeros((8, 128), F32))
        total = jnp.sum(jnp.sum(total, axis=0, keepdims=True), axis=1, keepdims=True)
        return -learn_rate / (jnp.sqrt(total) + norm_eps)

    def landing(s, half, src):
        return ag.at[r, half, src] if s == 0 else u[half].at[s - 1, src]

    def o_self(s, half):
        return pltpu.make_async_copy(ps.at[s, half, f], landing(s, half, f), loc.at[3 + s * 2 + half])

    def send_out(s, half, scale):
        def cut(d):
            y = pm[s, pl.ds(pl.multiple_of(d * 8, 8), 8), half * 256:(half + 1) * 256] * scale
            ps[s, half, d] = jnp.concatenate([y[:, 0:128], y[:, 128:256]], axis=0).astype(BF)

        def go(k, carry):
            d = (f + k) % N_FSDP
            cut(d)
            remote(ps.at[s, half, d], landing(s, half, f), o_send.at[s, half], o_recv.at[s, half], (d, r)).start()
            return carry

        lax.fori_loop(1, N_FSDP, go, 0, unroll=3)
        cut(f)
        o_self(s, half).start()

    def out_sent(s, half):
        most(s, half, ps, o_send, o_recv).wait_send()

    def wait_out(s, half):
        o_self(s, half).wait()
        most(s, half, ps, o_send, o_recv).wait_recv()

    def g_copy(part, kind, rep, a, n, to):
        here = ag.at[rep, part, pl.ds(a, n)]
        src = pk.at[part - 2] if part >= 2 and kind < 2 else here
        return remote(src, here, g_send.at[part], g_recv.at[part, min(kind, 2)], (f, to))

    def g_copies(part, kinds):
        every = (
            lambda: g_copy(part, 0, r, 0, 64, rt),
            lambda: g_copy(part, 1, r, 0, 64, lt),
            lambda: g_copy(part, 2, lt, 0, 32, rt),
            lambda: g_copy(part, 3, rt, 32, 32, lt),
        )
        return [every[k]() for k in kinds]

    def own_packed(half):
        return pltpu.make_async_copy(pk.at[half], ag.at[r, 2 + half], loc.at[9 + half])

    def gather_one(part):
        half = part % 2
        if part < 2:
            wait_out(0, half)
        else:
            wait_out(1, half)
            wait_out(2, half)

            def body(p, carry):
                pk[half, p] = u[half].reshape(128, *HALF)[tab[WHO, r * PACKED + p]]
                return carry

            lax.fori_loop(0, PACKED, body, 0, unroll=4)
            own_packed(half).start()
        for cp in g_copies(part, (0, 1)):
            cp.start()

    def gather_two(part):
        for k in (0, 1):
            g_copies(part, (k,))[0].wait_recv()
            g_copies(part, (k + 2,))[0].start()

    def gather_end(part):
        g_copy(part, 2, opp, 0, 64, rt).wait_recv()

    def adam():
        wait_b(4)
        wait_b(5)

        def one(c, k):
            lo = CHUNKS[c][0]
            return own32(c, r, k) + rb[0, lo + k].astype(F32) + rb[1, lo + k].astype(F32)

        def body(k, carry):
            total = jnp.concatenate([one(4, k), one(5, k)], axis=0)
            moment = moment_decay * vbuf[k] + (1.0 - moment_decay) * total * total
            step = total / (jnp.sqrt(moment) + adam_eps)
            acc[pl.ds(k, 1), :] = jnp.sum(step * step, axis=0, keepdims=True)
            return carry

        acc[pl.ds(80, 48), :] = jnp.zeros((48, 128), F32)
        lax.fori_loop(0, 80, body, 0, unroll=2)
        ones = jnp.ones((8, 128), F32)
        t1[...] = lax.dot_general(ones, acc[...], (((1,), (1,)), ((), ())),
                                  precision=lax.Precision.HIGHEST, preferred_element_type=F32)

    def n_parts(stage):
        return ((yc, t1, n1, t2), (z, t2, n2, t3), (r, t3, n3, None))[stage]

    def n_start(stage):
        me, tile, got, _ = n_parts(stage)
        for k in range(1, 4 if stage == 2 else 8):
            to = ((z * 8 + (yc + k) % 8, r), (((z + k) % 8) * 8 + yc, r), (f, (r + k) % 4))[stage]
            remote(tile, got.at[me], n_send.at[stage], n_recv.at[stage], to).start()
        got[me] = tile[...]

    def n_all(stage):
        got = n_parts(stage)[2]
        part = got.at[pl.ds(0, 3 if stage == 2 else 7)]
        return remote(part, part, n_send.at[stage], n_recv.at[stage], peer)

    def n_sum(stage):
        n_all(stage).wait_recv()
        _, _, got, out = n_parts(stage)
        if stage == 2:
            sq[...] = got[...]
        else:
            out[...] = jnp.sum(got[...], axis=0)

    fill_a(0)
    fill_a(1)
    for cp in loads:
        cp.wait()
    prep(1)
    pl.semaphore_wait(barrier, 3 + 7 + 7)
    for k in range(1, 8):
        pl.semaphore_signal(lines, inc=1, device_id=(z * 8 + (yc + k) % 8, r), device_id_type=MESH)
    send_a(0)
    fill_a(2)
    prep(2)
    step_b(0)
    send_a(1)
    fill_a(3)
    pl.semaphore_wait(lines, 7)
    step_p(0)
    step_b(1)
    send_a(2)
    step_p(1)
    step_b(2)
    send_a(3)
    step_b(3)
    fill_a(4)
    send_a(4)
    step_f(0)
    step_f(1)
    step_b(4)
    fill_a(5)
    prep(0)
    scale1 = product(1)
    send_out(1, 0, scale1)
    scale2 = product(2)
    send_out(2, 0, scale2)
    send_a(5)
    scale0 = product(0)
    out_sent(1, 0)
    send_out(0, 0, scale0)
    step_b(5)
    out_sent(2, 0)
    send_out(1, 1, scale1)
    gather_one(2)
    out_sent(0, 0)
    send_out(2, 1, scale2)
    gather_two(2)
    gather_one(0)
    out_sent(1, 1)
    send_out(0, 1, scale0)
    adam()
    n_start(0)
    gather_two(0)
    gather_one(3)
    n_sum(0)
    n_start(1)
    gather_two(3)
    n_sum(1)
    n_start(2)
    gather_one(1)
    gather_two(1)
    n_sum(2)
    for half in range(2):
        own_packed(half).wait()
    for part in (2, 3, 0, 1):
        gather_end(part)

    remote(sa, sa, x_send.at[0], x_recv.at[0, 0], (f, rt)).wait_send()
    for side in range(2):
        remote(sb.at[side], sb.at[side], x_send.at[1 + side], x_recv.at[0, 0], (f, rt)).wait_send()
    for s in range(SLOTS):
        for half in range(2):
            most(s, half, outgoing, a_send, a_recv).wait_send()
    out_sent(2, 1)
    out_sent(0, 1)
    for part in range(PARTS):
        three = ag.at[pl.ds(0, 3), part]
        remote(three, three, g_send.at[part], g_recv.at[part, 0], (f, rt)).wait_send()
    for stage in range(3):
        n_all(stage).wait_send()


def place(tab, ag, sq, out, norm):
    ones = jnp.where(lax.broadcasted_iota(jnp.int32, (8, 128), 0) == 0, 1.0, 0.0).astype(F32)
    for q in range(N_REP):
        rows = lax.dot_general(sq[q], ones, (((0,), (0,)), ((), ())),
                               precision=lax.Precision.HIGHEST, preferred_element_type=F32)
        norm[q * 128:(q + 1) * 128, :] = jnp.sqrt(rows)

    def line(i, carry):
        for q in range(N_REP):
            for j in range(QCOL):
                b = i * COLB + q * QCOL + j
                scale = norm[pl.ds(q * 128 + i * QCOL + j, 1), :]
                p = tab[POS, b]
                for half in range(2):
                    out[b, half] = (ag[p + half * 64].astype(F32) * scale).astype(BF)
        return carry

    lax.fori_loop(0, NBLK // COLB, line, 0)


def tables(owners, tab):
    row = owners[...].reshape(1, NBLK)
    sub = lax.broadcasted_iota(jnp.int32, (NBLK, NBLK), 0)
    lane = lax.broadcasted_iota(jnp.int32, (NBLK, NBLK), 1)

    def down(mask, value=1):
        return jnp.sum(jnp.where(mask, value, 0), axis=0, keepdims=True)

    def along(mask, value=1):
        return jnp.sum(jnp.where(mask, value, 0), axis=1, keepdims=True)

    col = along(sub == lane, row)
    same = col == row
    slot_c = along(same & (lane < sub))
    slot_r = down(same & (sub < lane))
    key_c, key_r = slot_c * N_FSDP + col, slot_r * N_FSDP + row
    alike = (slot_c & 3) == (slot_r & 3)
    rank_c = along(alike & (slot_r >= 4) & (key_r < key_c))
    rank_r = down(alike & (slot_c >= 4) & (key_c < key_r))
    code = jnp.where(slot_c < 4, key_c, 1024 + (slot_c & 3) * PACKED + rank_c)
    e = lax.broadcasted_iota(jnp.int32, (1, 256), 1)
    block = lax.broadcasted_iota(jnp.int32, (NBLK, 1), 0)
    a = e - 128
    line = sum(jnp.where(a >= QCOL * i, 1, 0) for i in range(1, 8))
    for t in range(N_REP):
        want = jnp.where(e < 64, 1024 + t * PACKED + e, t * N_FSDP + e - 64)
        found = down(code == want, block)
        mine = line * COLB + t * QCOL + a - line * QCOL
        tab[t:t + 1, 0:256] = jnp.where(e < 128, found, jnp.where(e < LIST, mine, 0))
    for s in (1, 2):
        tab[RANK + s - 1:RANK + s, 0:256] = down(key_c == s * 256 + e, rank_c)
    tab[WHO:WHO + 1, 0:256] = down(code == 1024 + e, ((slot_c >> 2) - 1) * N_FSDP + col)
    tab[POS:POS + 1, 0:NBLK] = (slot_r & 3) * 256 + jnp.where(slot_r < 4, row, 128 + rank_r)


def shards(gradients, second_moment, left_roots, right_roots, owners):
    grads = gradients.reshape(8, 8, 160, 128).transpose(0, 2, 1, 3).reshape(NBLK, 2, *HALF)
    second = second_moment.reshape(8, 8, 40, 128).transpose(0, 2, 1, 3).reshape(80, 32, 128)
    left = left_roots.reshape(SLOTS, 512, 512)
    right = right_roots.reshape(SLOTS, 512, 512)
    smem = pl.BlockSpec(memory_space=pltpu.SMEM)
    vmem = pl.BlockSpec(memory_space=pltpu.VMEM)
    hbm = pl.BlockSpec(memory_space=pl.ANY)
    dma = pltpu.SemaphoreType.DMA
    vm = pltpu.VMEM
    tab = pl.pallas_call(
        tables,
        out_shape=jax.ShapeDtypeStruct((8, 384), jnp.int32),
        in_specs=[vmem],
        out_specs=vmem,
        name="tables",
    )(owners)
    ag, sq = pl.pallas_call(
        exchange,
        out_shape=(
            jax.ShapeDtypeStruct((N_REP, PARTS, 64, *HALF), BF),
            jax.ShapeDtypeStruct((N_REP, 8, 128), F32),
        ),
        in_specs=[smem, vmem, hbm, hbm, hbm],
        out_specs=(hbm, vmem),
        scratch_shapes=[
            vm((ENTRIES, *HALF), BF), vm((ENTRIES, *HALF), BF),
            vm((2, ENTRIES, *HALF), BF), vm((2, ENTRIES, *HALF), BF),
            vm((2, PACKED, *HALF), BF), vm((2, PACKED, *HALF), BF),
            vm((SLOTS, 2, N_FSDP, *HALF), BF), vm((SLOTS, 2, N_FSDP, *HALF), BF),
            vm((512, 512), F32), vm((512, 512), BF),
            vm((SLOTS, 512, 512), F32), vm((SLOTS, 512, 512), F32),
            vm((SLOTS, 512, 512), BF), vm((SLOTS, 512, 512), BF),
            vm((SLOTS, 512, 512), BF), vm((SLOTS, 512, 512), BF), vm((80, 32, 128), F32),
            vm((SLOTS, 512, 512), F32), vm((SLOTS, 2, N_FSDP, *HALF), BF),
            vm((2, N_FSDP, *HALF), BF), vm((2, N_FSDP, *HALF), BF), vm((2, PACKED, *HALF), BF), vm((128, 128), F32),
            vm((8, 128), F32), vm((8, 128), F32), vm((8, 128), F32),
            vm((8, 8, 128), F32), vm((8, 8, 128), F32), vm((N_REP, 8, 128), F32),
            dma((3,)), dma((len(CHUNKS), 2)),
            dma((SLOTS, 2)), dma((SLOTS, 2)), dma((SLOTS, 2)), dma((SLOTS, 2)),
            dma((PARTS,)), dma((PARTS, 3)), dma((3,)), dma((3,)), dma((11,)), pltpu.SemaphoreType.REGULAR,
        ],
        compiler_params=pltpu.CompilerParams(collective_id=0, has_side_effects=True, vmem_limit_bytes=VMEM_LIMIT),
        name="exchange",
    )(tab, grads, second, left, right)
    out = pl.pallas_call(
        place,
        out_shape=jax.ShapeDtypeStruct((NBLK, 2, *HALF), BF),
        in_specs=[smem, vmem, vmem],
        out_specs=vmem,
        scratch_shapes=[vm((N_REP * 128, 128), F32)],
        compiler_params=pltpu.CompilerParams(vmem_limit_bytes=VMEM_LIMIT),
        name="place",
    )(tab, ag.reshape(N_REP * PARTS * 64, *HALF), sq)
    return out.reshape(8, 160, 8, 128).transpose(0, 2, 1, 3).reshape(8, 8, 20480)


def solution(mesh):
    return jax.shard_map(
        shards,
        mesh=mesh,
        in_specs=(
            P("rep", None, "fsdp", None),
            P(None, "fsdp", "rep"),
            P("fsdp", None, "rep", None, None),
            P("fsdp", None, "rep", None, None),
            P(),
        ),
        out_specs=P(None, "fsdp", None),
        check_vma=False,
    )
```

```python
import functools
import jax
import jax.numpy as jnp
from jax import lax
from jax.experimental import pallas as pl
from jax.experimental.pallas import tpu as pltpu
from jax.sharding import PartitionSpec as P

moment_decay = 0.999
adam_eps = 1e-08
norm_eps = 1e-06
learn_rate = 0.05

BF = jnp.bfloat16
F32 = jnp.float32
MESH = pl.DeviceIdType.MESH
N_FSDP = 64
N_REP = 4
NBLK = 320
SLOTS = 3
COLB = 40
QCOL = 10
HALF = (16, 128)
PACKED = 64
LIST = 208
CHUNKS = ((0, 64, 0, 0), (64, 64, 0, 1), (128, 64, 64, 0), (192, 64, 64, 1), (256, 80, 128, 0), (336, 80, 128, 1))
ENTRIES = 416
PARTS = 4
RANK, WHO, POS = 4, 6, 7
VMEM_LIMIT = 56 << 20


def split(x):
    hi = x.astype(BF)
    return hi, (x - hi.astype(F32)).astype(BF)


def mm(a, b):
    return jnp.dot(a, b, preferred_element_type=F32)


def exchange(tab, grads_in, second, left, right, ag, sq,
             grads, sa, ra, sb, rb, rbp0, rbp1, outgoing, arriving, g32, gbf, lbuf, rbuf, lhi, llo, rhi, rlo, vbuf,
             pm, ps, u0, u1, pk, acc, t1, t2, t3, n1, n2, n3,
             x_send, x_recv, a_send, a_recv, o_send, o_recv, g_send, g_recv, n_send, n_recv, loc, lines):
    f = lax.axis_index("fsdp")
    r = lax.axis_index("rep")
    rt, lt, opp = (r + 1) % 4, (r + 3) % 4, (r + 2) % 4
    z, yc = f // 8, f % 8
    peer = ((f + 1) % N_FSDP, r)
    rbp, u = (rbp0, rbp1), (u0, u1)

    grads_copy = pltpu.make_async_copy(grads_in, grads, loc.at[11])
    grads_copy.start()

    barrier = pltpu.get_barrier_semaphore()
    for other in (rt, lt, opp):
        pl.semaphore_signal(barrier, inc=1, device_id=(f, other), device_id_type=MESH)
    for k in range(1, 8):
        pl.semaphore_signal(barrier, inc=1, device_id=(z * 8 + (yc + k) % 8, r), device_id_type=MESH)
        pl.semaphore_signal(barrier, inc=1, device_id=(((z + k) % 8) * 8 + yc, r), device_id_type=MESH)

    loads = [pltpu.make_async_copy(left, lbuf, loc.at[0]), pltpu.make_async_copy(right, rbuf, loc.at[1]),
             pltpu.make_async_copy(second, vbuf, loc.at[2])]
    for cp in loads:
        cp.start()

    def own(c, target, k):
        return grads[tab[target, CHUNKS[c][2] + k], CHUNKS[c][3]]

    def own32(c, target, k):
        return own(c, target, k).astype(F32)

    def remote(src, dst, send, recv, to):
        return pltpu.make_async_remote_copy(src_ref=src, dst_ref=dst, send_sem=send, recv_sem=recv,
                                            device_id=to, device_id_type=MESH)

    def rb_at(c, side, k, n):
        return rbp[c].at[side, pl.ds(k, n)] if c < 2 else rb.at[side, pl.ds(CHUNKS[c][0] + k, n)]

    def x_copies(c, kinds):
        lo, n = CHUNKS[c][:2]
        h = n // 2
        first, last = pl.ds(lo, h), pl.ds(lo + h, h)
        right_to, left_to = (f, rt), (f, lt)
        one, two = x_recv.at[c, 0], x_recv.at[c, 1]
        every = (
            lambda: remote(sa.at[first], ra.at[first], x_send.at[0], one, right_to),
            lambda: remote(sa.at[last], ra.at[last], x_send.at[0], one, left_to),
            lambda: remote(sb.at[0, last], rb_at(c, 0, h, h), x_send.at[1], two, right_to),
            lambda: remote(sb.at[1, first], rb_at(c, 1, 0, h), x_send.at[2], two, left_to),
            lambda: remote(sb.at[0, first], rb_at(c, 0, 0, h), x_send.at[1], two, right_to),
            lambda: remote(sb.at[1, last], rb_at(c, 1, h, h), x_send.at[2], two, left_to),
        )
        return [every[k]() for k in kinds]

    def fill_a(c):
        lo, n = CHUNKS[c][:2]
        h = n // 2

        def body(k, carry):
            sa[lo + k] = own(c, opp, k)
            sa[lo + h + k] = own(c, opp, h + k)
            sb[0, lo + h + k] = own(c, rt, h + k)
            sb[1, lo + k] = own(c, lt, k)
            return carry

        lax.fori_loop(0, h, body, 0, unroll=4)

    def send_a(c):
        for cp in x_copies(c, (0, 1, 2, 3)):
            cp.start()

    def step_b(c):
        lo, n = CHUNKS[c][:2]
        h = n // 2
        both = pl.ds(lo, n)
        remote(sa.at[both], ra.at[both], x_send.at[0], x_recv.at[c, 0], (f, rt)).wait_recv()

        def body(k, carry):
            e, g = lo + k, lo + h + k
            sb[0, e] = (own32(c, rt, k) + ra[e].astype(F32)).astype(BF)
            sb[1, g] = (own32(c, lt, h + k) + ra[g].astype(F32)).astype(BF)
            return carry

        lax.fori_loop(0, h, body, 0, unroll=4)
        for cp in x_copies(c, (4, 5)):
            cp.start()

    def wait_b(c):
        lo, n = CHUNKS[c][:2]
        both = sb.at[:, pl.ds(lo, n)]
        remote(both, both, x_send.at[1], x_recv.at[c, 1], (f, rt)).wait_recv()

    def most(s, half, buf, send, recv):
        part = buf.at[s, half, pl.ds(0, N_FSDP - 1)]
        return remote(part, part, send.at[s, half], recv.at[s, half], peer)

    def to_owners(s, half, total):
        def body(k, carry):
            d = (f + k) % N_FSDP
            outgoing[s, half, d] = total(d).astype(BF)
            remote(outgoing.at[s, half, d], arriving.at[s, half, f], a_send.at[s, half], a_recv.at[s, half],
                   (d, r)).start()
            return carry

        lax.fori_loop(1, N_FSDP, body, 0, unroll=3)
        arriving[s, half, f] = total(f).astype(BF)

    def step_f(half):
        c = 2 + half
        lo = CHUNKS[c][0]
        wait_b(c)
        to_owners(0, half, lambda d: own32(c, r, d) + rb[0, lo + d].astype(F32) + rb[1, lo + d].astype(F32))

    def step_p(half):
        got = rbp[half]
        wait_b(half)
        for s in (1, 2):
            def total(d, s=s):
                p = tab[RANK + s - 1, r * N_FSDP + d]
                return own32(half, r, p) + got[0, p].astype(F32) + got[1, p].astype(F32)

            to_owners(s, half, total)

    def prep(s):
        def body(k, carry):
            rows = pl.ds(pl.multiple_of(k * 64, 64), 64)
            lhi[s, rows, :], llo[s, rows, :] = split(lbuf[s, rows, :])
            rhi[s, rows, :], rlo[s, rows, :] = split(rbuf[s, rows, :])
            return carry

        lax.fori_loop(0, 8, body, 0)

    def product(s):
        for half in range(2):
            most(s, half, arriving, a_send, a_recv).wait_recv()

            def gather(m, carry, half=half):
                x = arriving[s, half, m].astype(F32)
                for t in range(2):
                    cols = slice(half * 256 + t * 128, half * 256 + (t + 1) * 128)
                    g32[pl.ds(pl.multiple_of(m * 8, 8), 8), cols] = x[t * 8:(t + 1) * 8]
                return carry

            lax.fori_loop(0, N_FSDP, gather, 0, unroll=4)
        gbf[...] = g32[...].astype(BF)

        def rows_of(k, total):
            rows = pl.ds(pl.multiple_of(k * 128, 128), 128)
            half_way = mm(lhi[s, rows, :], gbf[...]) + mm(llo[s, rows, :], gbf[...])
            hhi, hlo = split(half_way)
            p = mm(hhi, rhi[s]) + (mm(hlo, rhi[s]) + mm(hhi, rlo[s]))
            pm[s, rows, :] = p
            q = p * p
            q = q.reshape(16, 8, 512).sum(axis=0)
            return total + (q[:, 0:128] + q[:, 128:256] + q[:, 256:384] + q[:, 384:512])

        total = lax.fori_loop(0, 4, rows_of, jnp.zeros((8, 128), F32))
        total = jnp.sum(jnp.sum(total, axis=0, keepdims=True), axis=1, keepdims=True)
        return -learn_rate / (jnp.sqrt(total) + norm_eps)

    def landing(s, half, src):
        return ag.at[r, half, src] if s == 0 else u[half].at[s - 1, src]

    def o_self(s, half):
        return pltpu.make_async_copy(ps.at[s, half, f], landing(s, half, f), loc.at[3 + s * 2 + half])

    def send_out(s, half, scale):
        def cut(d):
            y = pm[s, pl.ds(pl.multiple_of(d * 8, 8), 8), half * 256:(half + 1) * 256] * scale
            ps[s, half, d] = jnp.concatenate([y[:, 0:128], y[:, 128:256]], axis=0).astype(BF)

        def go(k, carry):
            d = (f + k) % N_FSDP
            cut(d)
            remote(ps.at[s, half, d], landing(s, half, f), o_send.at[s, half], o_recv.at[s, half], (d, r)).start()
            return carry

        lax.fori_loop(1, N_FSDP, go, 0, unroll=3)
        cut(f)
        o_self(s, half).start()

    def out_sent(s, half):
        most(s, half, ps, o_send, o_recv).wait_send()

    def wait_out(s, half):
        o_self(s, half).wait()
        most(s, half, ps, o_send, o_recv).wait_recv()

    def g_copy(part, kind, rep, a, n, to):
        here = ag.at[rep, part, pl.ds(a, n)]
        src = pk.at[part - 2] if part >= 2 and kind < 2 else here
        return remote(src, here, g_send.at[part], g_recv.at[part, min(kind, 2)], (f, to))

    def g_copies(part, kinds):
        every = (
            lambda: g_copy(part, 0, r, 0, 64, rt),
            lambda: g_copy(part, 1, r, 0, 64, lt),
            lambda: g_copy(part, 2, lt, 0, 32, rt),
            lambda: g_copy(part, 3, rt, 32, 32, lt),
        )
        return [every[k]() for k in kinds]

    def own_packed(half):
        return pltpu.make_async_copy(pk.at[half], ag.at[r, 2 + half], loc.at[9 + half])

    def gather_one(part):
        half = part % 2
        if part < 2:
            wait_out(0, half)
        else:
            wait_out(1, half)
            wait_out(2, half)

            def body(p, carry):
                pk[half, p] = u[half].reshape(128, *HALF)[tab[WHO, r * PACKED + p]]
                return carry

            lax.fori_loop(0, PACKED, body, 0, unroll=4)
            own_packed(half).start()
        for cp in g_copies(part, (0, 1)):
            cp.start()

    def gather_two(part):
        for k in (0, 1):
            g_copies(part, (k,))[0].wait_recv()
            g_copies(part, (k + 2,))[0].start()

    def gather_end(part):
        g_copy(part, 2, opp, 0, 64, rt).wait_recv()

    def adam():
        wait_b(4)
        wait_b(5)

        def one(c, k):
            lo = CHUNKS[c][0]
            return own32(c, r, k) + rb[0, lo + k].astype(F32) + rb[1, lo + k].astype(F32)

        def body(k, carry):
            total = jnp.concatenate([one(4, k), one(5, k)], axis=0)
            moment = moment_decay * vbuf[k] + (1.0 - moment_decay) * total * total
            step = total / (jnp.sqrt(moment) + adam_eps)
            acc[pl.ds(k, 1), :] = jnp.sum(step * step, axis=0, keepdims=True)
            return carry

        acc[pl.ds(80, 48), :] = jnp.zeros((48, 128), F32)
        lax.fori_loop(0, 80, body, 0, unroll=2)
        ones = jnp.ones((8, 128), F32)
        t1[...] = lax.dot_general(ones, acc[...], (((1,), (1,)), ((), ())),
                                  precision=lax.Precision.HIGHEST, preferred_element_type=F32)

    def n_parts(stage):
        return ((yc, t1, n1, t2), (z, t2, n2, t3), (r, t3, n3, None))[stage]

    def n_start(stage):
        me, tile, got, _ = n_parts(stage)
        for k in range(1, 4 if stage == 2 else 8):
            to = ((z * 8 + (yc + k) % 8, r), (((z + k) % 8) * 8 + yc, r), (f, (r + k) % 4))[stage]
            remote(tile, got.at[me], n_send.at[stage], n_recv.at[stage], to).start()
        got[me] = tile[...]

    def n_all(stage):
        got = n_parts(stage)[2]
        part = got.at[pl.ds(0, 3 if stage == 2 else 7)]
        return remote(part, part, n_send.at[stage], n_recv.at[stage], peer)

    def n_sum(stage):
        n_all(stage).wait_recv()
        _, _, got, out = n_parts(stage)
        if stage == 2:
            sq[...] = got[...]
        else:
            out[...] = jnp.sum(got[...], axis=0)

    grads_copy.wait()
    fill_a(0)
    pl.semaphore_wait(barrier, 3 + 7 + 7)
    send_a(0)
    for k in range(1, 8):
        pl.semaphore_signal(lines, inc=1, device_id=(z * 8 + (yc + k) % 8, r), device_id_type=MESH)
    fill_a(1)
    for cp in loads:
        cp.wait()
    prep(1)
    step_b(0)
    send_a(1)
    fill_a(2)
    prep(2)
    pl.semaphore_wait(lines, 7)
    step_p(0)
    step_b(1)
    fill_a(3)
    send_a(2)
    step_p(1)
    step_b(2)
    send_a(3)
    fill_a(4)
    prep(0)
    step_b(3)
    send_a(4)
    step_f(0)
    fill_a(5)
    step_f(1)
    scale1 = product(1)
    send_out(1, 0, scale1)
    scale2 = product(2)
    send_out(2, 0, scale2)
    step_b(4)
    send_a(5)
    scale0 = product(0)
    out_sent(1, 0)
    send_out(0, 0, scale0)
    step_b(5)
    out_sent(2, 0)
    send_out(0, 1, scale0)
    gather_one(2)
    out_sent(0, 0)
    send_out(1, 1, scale1)
    gather_two(2)
    gather_one(0)
    out_sent(0, 1)
    send_out(2, 1, scale2)
    adam()
    n_start(0)
    gather_two(0)
    gather_one(1)
    n_sum(0)
    n_start(1)
    gather_two(1)
    n_sum(1)
    n_start(2)
    gather_one(3)
    gather_two(3)
    n_sum(2)
    for half in range(2):
        own_packed(half).wait()
    for part in (2, 3, 0, 1):
        gather_end(part)

    remote(sa, sa, x_send.at[0], x_recv.at[0, 0], (f, rt)).wait_send()
    for side in range(2):
        remote(sb.at[side], sb.at[side], x_send.at[1 + side], x_recv.at[0, 0], (f, rt)).wait_send()
    for s in range(SLOTS):
        for half in range(2):
            most(s, half, outgoing, a_send, a_recv).wait_send()
    out_sent(1, 1)
    out_sent(2, 1)
    for part in range(PARTS):
        three = ag.at[pl.ds(0, 3), part]
        remote(three, three, g_send.at[part], g_recv.at[part, 0], (f, rt)).wait_send()
    for stage in range(3):
        n_all(stage).wait_send()


def place(tab, ag, sq, out, norm, buf, res, came, left):
    loads = [[pltpu.make_async_copy(ag.at[:, kind * 2 + half], buf.at[half, :, kind], came.at[half, kind])
              for kind in range(2)] for half in range(2)]
    for pair in loads:
        for cp in pair:
            cp.start()
    ones = jnp.where(lax.broadcasted_iota(jnp.int32, (8, 128), 0) == 0, 1.0, 0.0).astype(F32)
    for q in range(N_REP):
        rows = lax.dot_general(sq[q], ones, (((0,), (0,)), ((), ())),
                               precision=lax.Precision.HIGHEST, preferred_element_type=F32)
        norm[q * 128:(q + 1) * 128, :] = jnp.sqrt(rows)

    for half in range(2):
        for cp in loads[half]:
            cp.wait()
        entries = buf.at[half].reshape(N_REP * 128, *HALF)

        def line(i, carry, half=half, entries=entries):
            for q in range(N_REP):
                for j in range(QCOL):
                    b = i * COLB + q * QCOL + j
                    scale = norm[pl.ds(q * 128 + i * QCOL + j, 1), :]
                    res[half, b] = (entries[tab[POS, b]].astype(F32) * scale).astype(BF)
            mine = pl.ds(i * COLB, COLB)
            pltpu.make_async_copy(res.at[half, mine], out.at[mine, half], left.at[half]).start()
            return carry

        lax.fori_loop(0, NBLK // COLB, line, 0)
    for half in range(2):
        pltpu.make_async_copy(res.at[half], out.at[:, half], left.at[half]).wait()


def tables(owners, tab):
    row = owners[...].reshape(1, NBLK)
    sub = lax.broadcasted_iota(jnp.int32, (NBLK, NBLK), 0)
    lane = lax.broadcasted_iota(jnp.int32, (NBLK, NBLK), 1)

    def down(mask, value=1):
        return jnp.sum(jnp.where(mask, value, 0), axis=0, keepdims=True)

    def along(mask, value=1):
        return jnp.sum(jnp.where(mask, value, 0), axis=1, keepdims=True)

    col = along(sub == lane, row)
    same = col == row
    slot_c = along(same & (lane < sub))
    slot_r = down(same & (sub < lane))
    key_c, key_r = slot_c * N_FSDP + col, slot_r * N_FSDP + row
    alike = (slot_c & 3) == (slot_r & 3)
    rank_c = along(alike & (slot_r >= 4) & (key_r < key_c))
    rank_r = down(alike & (slot_c >= 4) & (key_c < key_r))
    code = jnp.where(slot_c < 4, key_c, 1024 + (slot_c & 3) * PACKED + rank_c)
    e = lax.broadcasted_iota(jnp.int32, (1, 256), 1)
    block = lax.broadcasted_iota(jnp.int32, (NBLK, 1), 0)
    a = e - 128
    line = sum(jnp.where(a >= QCOL * i, 1, 0) for i in range(1, 8))
    for t in range(N_REP):
        want = jnp.where(e < 64, 1024 + t * PACKED + e, t * N_FSDP + e - 64)
        found = down(code == want, block)
        mine = line * COLB + t * QCOL + a - line * QCOL
        tab[t:t + 1, 0:256] = jnp.where(e < 128, found, jnp.where(e < LIST, mine, 0))
    for s in (1, 2):
        tab[RANK + s - 1:RANK + s, 0:256] = down(key_c == s * 256 + e, rank_c)
    tab[WHO:WHO + 1, 0:256] = down(code == 1024 + e, ((slot_c >> 2) - 1) * N_FSDP + col)
    tab[POS:POS + 1, 0:NBLK] = (slot_r & 3) * 128 + jnp.where(slot_r < 4, row, 64 + rank_r)


def shards(gradients, second_moment, left_roots, right_roots, owners):
    grads = gradients.reshape(8, 8, 160, 128).transpose(0, 2, 1, 3).reshape(NBLK, 2, *HALF)
    second = second_moment.reshape(8, 8, 40, 128).transpose(0, 2, 1, 3).reshape(80, 32, 128)
    left = left_roots.reshape(SLOTS, 512, 512)
    right = right_roots.reshape(SLOTS, 512, 512)
    smem = pl.BlockSpec(memory_space=pltpu.SMEM)
    vmem = pl.BlockSpec(memory_space=pltpu.VMEM)
    hbm = pl.BlockSpec(memory_space=pl.ANY)
    dma = pltpu.SemaphoreType.DMA
    vm = pltpu.VMEM
    tab = pl.pallas_call(
        tables,
        out_shape=jax.ShapeDtypeStruct((8, 384), jnp.int32),
        in_specs=[vmem],
        out_specs=vmem,
        name="tables",
    )(owners)
    ag, sq = pl.pallas_call(
        exchange,
        out_shape=(
            jax.ShapeDtypeStruct((N_REP, PARTS, 64, *HALF), BF),
            jax.ShapeDtypeStruct((N_REP, 8, 128), F32),
        ),
        in_specs=[smem, hbm, hbm, hbm, hbm],
        out_specs=(hbm, vmem),
        scratch_shapes=[
            vm((NBLK, 2, *HALF), BF), vm((ENTRIES, *HALF), BF), vm((ENTRIES, *HALF), BF),
            vm((2, ENTRIES, *HALF), BF), vm((2, ENTRIES, *HALF), BF),
            vm((2, PACKED, *HALF), BF), vm((2, PACKED, *HALF), BF),
            vm((SLOTS, 2, N_FSDP, *HALF), BF), vm((SLOTS, 2, N_FSDP, *HALF), BF),
            vm((512, 512), F32), vm((512, 512), BF),
            vm((SLOTS, 512, 512), F32), vm((SLOTS, 512, 512), F32),
            vm((SLOTS, 512, 512), BF), vm((SLOTS, 512, 512), BF),
            vm((SLOTS, 512, 512), BF), vm((SLOTS, 512, 512), BF), vm((80, 32, 128), F32),
            vm((SLOTS, 512, 512), F32), vm((SLOTS, 2, N_FSDP, *HALF), BF),
            vm((2, N_FSDP, *HALF), BF), vm((2, N_FSDP, *HALF), BF), vm((2, PACKED, *HALF), BF), vm((128, 128), F32),
            vm((8, 128), F32), vm((8, 128), F32), vm((8, 128), F32),
            vm((8, 8, 128), F32), vm((8, 8, 128), F32), vm((N_REP, 8, 128), F32),
            dma((3,)), dma((len(CHUNKS), 2)),
            dma((SLOTS, 2)), dma((SLOTS, 2)), dma((SLOTS, 2)), dma((SLOTS, 2)),
            dma((PARTS,)), dma((PARTS, 3)), dma((3,)), dma((3,)), dma((12,)), pltpu.SemaphoreType.REGULAR,
        ],
        compiler_params=pltpu.CompilerParams(collective_id=0, has_side_effects=True, vmem_limit_bytes=VMEM_LIMIT),
        name="exchange",
    )(tab, grads, second, left, right)
    out = pl.pallas_call(
        place,
        out_shape=jax.ShapeDtypeStruct((NBLK, 2, *HALF), BF),
        in_specs=[smem, hbm, vmem],
        out_specs=hbm,
        scratch_shapes=[vm((N_REP * 128, 128), F32), vm((2, N_REP, 2, 64, *HALF), BF), vm((2, NBLK, *HALF), BF),
                        dma((2, 2)), dma((2,))],
        compiler_params=pltpu.CompilerParams(vmem_limit_bytes=VMEM_LIMIT),
        name="place",
    )(tab, ag, sq)
    return out.reshape(8, 160, 8, 128).transpose(0, 2, 1, 3).reshape(8, 8, 20480)


def solution(mesh):
    return jax.shard_map(
        shards,
        mesh=mesh,
        in_specs=(
            P("rep", None, "fsdp", None),
            P(None, "fsdp", "rep"),
            P("fsdp", None, "rep", None, None),
            P("fsdp", None, "rep", None, None),
            P(),
        ),
        out_specs=P(None, "fsdp", None),
        check_vma=False,
    )
```

```python
import functools
import jax
import jax.numpy as jnp
from jax import lax
from jax.experimental import pallas as pl
from jax.experimental.pallas import tpu as pltpu
from jax.sharding import PartitionSpec as P

moment_decay = 0.999
adam_eps = 1e-08
norm_eps = 1e-06
learn_rate = 0.05

BF = jnp.bfloat16
F32 = jnp.float32
MESH = pl.DeviceIdType.MESH
N_FSDP = 64
N_REP = 4
NBLK = 320
SLOTS = 3
COLB = 40
QCOL = 10
HALF = (16, 128)
PACKED = 64
LIST = 208
CHUNKS = ((0, 64, 0, 0), (64, 64, 0, 1), (128, 64, 64, 0), (192, 64, 64, 1), (256, 80, 128, 0), (336, 80, 128, 1))
ENTRIES = 416
PARTS = 4
RANK, WHO, POS = 4, 6, 7
VMEM_LIMIT = 56 << 20


def split(x):
    hi = x.astype(BF)
    return hi, (x - hi.astype(F32)).astype(BF)


def mm(a, b):
    return jnp.dot(a, b, preferred_element_type=F32)


def exchange(tab, grads_in, second, left, right, ag, sq,
             grads, sa, ra, sb, rb, rbp0, rbp1, outgoing, arriving, g32, gbf, lbuf, rbuf, lhi, llo, rhi, rlo, vbuf,
             pm, ps, u0, u1, pk, acc, t1, t2, t3, n1, n2, n3,
             x_send, x_recv, a_send, a_recv, o_send, o_recv, g_send, g_recv, n_send, n_recv, loc, lines):
    f = lax.axis_index("fsdp")
    r = lax.axis_index("rep")
    rt, lt, opp = (r + 1) % 4, (r + 3) % 4, (r + 2) % 4
    z, yc = f // 8, f % 8
    peer = ((f + 1) % N_FSDP, r)
    rbp, u = (rbp0, rbp1), (u0, u1)

    grads_copy = pltpu.make_async_copy(grads_in, grads, loc.at[11])
    grads_copy.start()

    barrier = pltpu.get_barrier_semaphore()
    for other in (rt, lt, opp):
        pl.semaphore_signal(barrier, inc=1, device_id=(f, other), device_id_type=MESH)
    for k in range(1, 8):
        pl.semaphore_signal(barrier, inc=1, device_id=(z * 8 + (yc + k) % 8, r), device_id_type=MESH)
        pl.semaphore_signal(barrier, inc=1, device_id=(((z + k) % 8) * 8 + yc, r), device_id_type=MESH)

    loads = [pltpu.make_async_copy(left, lbuf, loc.at[0]), pltpu.make_async_copy(right, rbuf, loc.at[1]),
             pltpu.make_async_copy(second, vbuf, loc.at[2])]
    for cp in loads:
        cp.start()

    def own(c, target, k):
        return grads[tab[target, CHUNKS[c][2] + k], CHUNKS[c][3]]

    def own32(c, target, k):
        return own(c, target, k).astype(F32)

    def remote(src, dst, send, recv, to):
        return pltpu.make_async_remote_copy(src_ref=src, dst_ref=dst, send_sem=send, recv_sem=recv,
                                            device_id=to, device_id_type=MESH)

    def rb_at(c, side, k, n):
        return rbp[c].at[side, pl.ds(k, n)] if c < 2 else rb.at[side, pl.ds(CHUNKS[c][0] + k, n)]

    def x_copies(c, kinds):
        lo, n = CHUNKS[c][:2]
        h = n // 2
        first, last = pl.ds(lo, h), pl.ds(lo + h, h)
        right_to, left_to = (f, rt), (f, lt)
        one, two = x_recv.at[c, 0], x_recv.at[c, 1]
        every = (
            lambda: remote(sa.at[first], ra.at[first], x_send.at[0], one, right_to),
            lambda: remote(sa.at[last], ra.at[last], x_send.at[0], one, left_to),
            lambda: remote(sb.at[0, last], rb_at(c, 0, h, h), x_send.at[1], two, right_to),
            lambda: remote(sb.at[1, first], rb_at(c, 1, 0, h), x_send.at[2], two, left_to),
            lambda: remote(sb.at[0, first], rb_at(c, 0, 0, h), x_send.at[1], two, right_to),
            lambda: remote(sb.at[1, last], rb_at(c, 1, h, h), x_send.at[2], two, left_to),
        )
        return [every[k]() for k in kinds]

    def fill_a(c):
        lo, n = CHUNKS[c][:2]
        h = n // 2

        def body(k, carry):
            sa[lo + k] = own(c, opp, k)
            sa[lo + h + k] = own(c, opp, h + k)
            sb[0, lo + h + k] = own(c, rt, h + k)
            sb[1, lo + k] = own(c, lt, k)
            return carry

        lax.fori_loop(0, h, body, 0, unroll=4)

    def send_a(c):
        for cp in x_copies(c, (0, 1, 2, 3)):
            cp.start()

    def step_b(c):
        lo, n = CHUNKS[c][:2]
        h = n // 2
        both = pl.ds(lo, n)
        remote(sa.at[both], ra.at[both], x_send.at[0], x_recv.at[c, 0], (f, rt)).wait_recv()

        def body(k, carry):
            e, g = lo + k, lo + h + k
            sb[0, e] = (own32(c, rt, k) + ra[e].astype(F32)).astype(BF)
            sb[1, g] = (own32(c, lt, h + k) + ra[g].astype(F32)).astype(BF)
            return carry

        lax.fori_loop(0, h, body, 0, unroll=4)
        for cp in x_copies(c, (4, 5)):
            cp.start()

    def wait_b(c):
        lo, n = CHUNKS[c][:2]
        both = sb.at[:, pl.ds(lo, n)]
        remote(both, both, x_send.at[1], x_recv.at[c, 1], (f, rt)).wait_recv()

    def most(s, half, buf, send, recv):
        part = buf.at[s, half, pl.ds(0, N_FSDP - 1)]
        return remote(part, part, send.at[s, half], recv.at[s, half], peer)

    def to_owners(s, half, total):
        def body(k, carry):
            d = (f + k) % N_FSDP
            outgoing[s, half, d] = total(d).astype(BF)
            remote(outgoing.at[s, half, d], arriving.at[s, half, f], a_send.at[s, half], a_recv.at[s, half],
                   (d, r)).start()
            return carry

        lax.fori_loop(1, N_FSDP, body, 0, unroll=3)
        arriving[s, half, f] = total(f).astype(BF)

    def step_f(half):
        c = 2 + half
        lo = CHUNKS[c][0]
        wait_b(c)
        to_owners(0, half, lambda d: own32(c, r, d) + rb[0, lo + d].astype(F32) + rb[1, lo + d].astype(F32))

    def step_p(half):
        got = rbp[half]
        wait_b(half)
        for s in (1, 2):
            def total(d, s=s):
                p = tab[RANK + s - 1, r * N_FSDP + d]
                return own32(half, r, p) + got[0, p].astype(F32) + got[1, p].astype(F32)

            to_owners(s, half, total)

    def prep(s):
        def body(k, carry):
            rows = pl.ds(pl.multiple_of(k * 64, 64), 64)
            lhi[s, rows, :], llo[s, rows, :] = split(lbuf[s, rows, :])
            rhi[s, rows, :], rlo[s, rows, :] = split(rbuf[s, rows, :])
            return carry

        lax.fori_loop(0, 8, body, 0)

    def product(s):
        for half in range(2):
            most(s, half, arriving, a_send, a_recv).wait_recv()

            def gather(m, carry, half=half):
                x = arriving[s, half, m].astype(F32)
                for t in range(2):
                    cols = slice(half * 256 + t * 128, half * 256 + (t + 1) * 128)
                    g32[pl.ds(pl.multiple_of(m * 8, 8), 8), cols] = x[t * 8:(t + 1) * 8]
                return carry

            lax.fori_loop(0, N_FSDP, gather, 0, unroll=4)
        gbf[...] = g32[...].astype(BF)

        def rows_of(k, total):
            rows = pl.ds(pl.multiple_of(k * 128, 128), 128)
            half_way = mm(lhi[s, rows, :], gbf[...]) + mm(llo[s, rows, :], gbf[...])
            hhi, hlo = split(half_way)
            p = mm(hhi, rhi[s]) + (mm(hlo, rhi[s]) + mm(hhi, rlo[s]))
            pm[s, rows, :] = p
            q = p * p
            q = q.reshape(16, 8, 512).sum(axis=0)
            return total + (q[:, 0:128] + q[:, 128:256] + q[:, 256:384] + q[:, 384:512])

        total = lax.fori_loop(0, 4, rows_of, jnp.zeros((8, 128), F32))
        total = jnp.sum(jnp.sum(total, axis=0, keepdims=True), axis=1, keepdims=True)
        return -learn_rate / (jnp.sqrt(total) + norm_eps)

    def landing(s, half, src):
        return ag.at[r, half, src] if s == 0 else u[half].at[s - 1, src]

    def o_self(s, half):
        return pltpu.make_async_copy(ps.at[s, half, f], landing(s, half, f), loc.at[3 + s * 2 + half])

    def send_out(s, half, scale):
        def cut(d):
            y = pm[s, pl.ds(pl.multiple_of(d * 8, 8), 8), half * 256:(half + 1) * 256] * scale
            ps[s, half, d] = jnp.concatenate([y[:, 0:128], y[:, 128:256]], axis=0).astype(BF)

        def go(k, carry):
            d = (f + k) % N_FSDP
            cut(d)
            remote(ps.at[s, half, d], landing(s, half, f), o_send.at[s, half], o_recv.at[s, half], (d, r)).start()
            return carry

        lax.fori_loop(1, N_FSDP, go, 0, unroll=3)
        cut(f)
        o_self(s, half).start()

    def out_sent(s, half):
        most(s, half, ps, o_send, o_recv).wait_send()

    def wait_out(s, half):
        o_self(s, half).wait()
        most(s, half, ps, o_send, o_recv).wait_recv()

    def g_copy(part, kind, rep, a, n, to):
        here = ag.at[rep, part, pl.ds(a, n)]
        src = pk.at[part - 2] if part >= 2 and kind < 2 else here
        return remote(src, here, g_send.at[part], g_recv.at[part, min(kind, 2)], (f, to))

    def g_copies(part, kinds):
        every = (
            lambda: g_copy(part, 0, r, 0, 64, rt),
            lambda: g_copy(part, 1, r, 0, 64, lt),
            lambda: g_copy(part, 2, lt, 0, 32, rt),
            lambda: g_copy(part, 3, rt, 32, 32, lt),
        )
        return [every[k]() for k in kinds]

    def own_packed(half):
        return pltpu.make_async_copy(pk.at[half], ag.at[r, 2 + half], loc.at[9 + half])

    def gather_one(part):
        half = part % 2
        if part < 2:
            wait_out(0, half)
        else:
            wait_out(1, half)
            wait_out(2, half)

            def body(p, carry):
                pk[half, p] = u[half].reshape(128, *HALF)[tab[WHO, r * PACKED + p]]
                return carry

            lax.fori_loop(0, PACKED, body, 0, unroll=4)
            own_packed(half).start()
        for cp in g_copies(part, (0, 1)):
            cp.start()

    def gather_two(part):
        for k in (0, 1):
            g_copies(part, (k,))[0].wait_recv()
            g_copies(part, (k + 2,))[0].start()

    def gather_end(part):
        g_copy(part, 2, opp, 0, 64, rt).wait_recv()

    def adam():
        wait_b(4)
        wait_b(5)

        def one(c, k):
            lo = CHUNKS[c][0]
            return own32(c, r, k) + rb[0, lo + k].astype(F32) + rb[1, lo + k].astype(F32)

        def body(k, carry):
            total = jnp.concatenate([one(4, k), one(5, k)], axis=0)
            moment = moment_decay * vbuf[k] + (1.0 - moment_decay) * total * total
            step = total / (jnp.sqrt(moment) + adam_eps)
            acc[pl.ds(k, 1), :] = jnp.sum(step * step, axis=0, keepdims=True)
            return carry

        acc[pl.ds(80, 48), :] = jnp.zeros((48, 128), F32)
        lax.fori_loop(0, 80, body, 0, unroll=2)
        ones = jnp.ones((8, 128), F32)
        t1[...] = lax.dot_general(ones, acc[...], (((1,), (1,)), ((), ())),
                                  precision=lax.Precision.HIGHEST, preferred_element_type=F32)

    def n_parts(stage):
        return ((yc, t1, n1, t2), (z, t2, n2, t3), (r, t3, n3, None))[stage]

    def n_start(stage):
        me, tile, got, _ = n_parts(stage)
        for k in range(1, 4 if stage == 2 else 8):
            to = ((z * 8 + (yc + k) % 8, r), (((z + k) % 8) * 8 + yc, r), (f, (r + k) % 4))[stage]
            remote(tile, got.at[me], n_send.at[stage], n_recv.at[stage], to).start()
        got[me] = tile[...]

    def n_all(stage):
        got = n_parts(stage)[2]
        part = got.at[pl.ds(0, 3 if stage == 2 else 7)]
        return remote(part, part, n_send.at[stage], n_recv.at[stage], peer)

    def n_sum(stage):
        n_all(stage).wait_recv()
        _, _, got, out = n_parts(stage)
        if stage == 2:
            sq[...] = got[...]
        else:
            out[...] = jnp.sum(got[...], axis=0)

    grads_copy.wait()
    fill_a(0)
    pl.semaphore_wait(barrier, 3 + 7 + 7)
    send_a(0)
    for k in range(1, 8):
        pl.semaphore_signal(lines, inc=1, device_id=(z * 8 + (yc + k) % 8, r), device_id_type=MESH)
    fill_a(1)
    for cp in loads:
        cp.wait()
    prep(1)
    step_b(0)
    send_a(1)
    fill_a(2)
    prep(2)
    pl.semaphore_wait(lines, 7)
    step_p(0)
    step_b(1)
    fill_a(3)
    send_a(2)
    step_p(1)
    step_b(2)
    send_a(3)
    fill_a(4)
    prep(0)
    step_b(3)
    send_a(4)
    step_f(0)
    fill_a(5)
    step_f(1)
    scale1 = product(1)
    send_out(1, 0, scale1)
    scale2 = product(2)
    send_out(2, 0, scale2)
    step_b(4)
    send_a(5)
    scale0 = product(0)
    out_sent(1, 0)
    send_out(0, 0, scale0)
    step_b(5)
    out_sent(2, 0)
    send_out(0, 1, scale0)
    gather_one(2)
    out_sent(0, 0)
    send_out(1, 1, scale1)
    adam()
    n_start(0)
    gather_two(2)
    gather_one(0)
    out_sent(0, 1)
    send_out(2, 1, scale2)
    n_sum(0)
    n_start(1)
    gather_two(0)
    n_sum(1)
    n_start(2)
    gather_one(1)
    gather_two(1)
    gather_one(3)
    gather_two(3)
    n_sum(2)
    for half in range(2):
        own_packed(half).wait()
    for part in (2, 3, 0, 1):
        gather_end(part)

    remote(sa, sa, x_send.at[0], x_recv.at[0, 0], (f, rt)).wait_send()
    for side in range(2):
        remote(sb.at[side], sb.at[side], x_send.at[1 + side], x_recv.at[0, 0], (f, rt)).wait_send()
    for s in range(SLOTS):
        for half in range(2):
            most(s, half, outgoing, a_send, a_recv).wait_send()
    out_sent(1, 1)
    out_sent(2, 1)
    for part in range(PARTS):
        three = ag.at[pl.ds(0, 3), part]
        remote(three, three, g_send.at[part], g_recv.at[part, 0], (f, rt)).wait_send()
    for stage in range(3):
        n_all(stage).wait_send()


def place(tab, ag, sq, out, norm, buf, res, came, left):
    loads = [[pltpu.make_async_copy(ag.at[:, kind * 2 + half], buf.at[half, :, kind], came.at[half, kind])
              for kind in range(2)] for half in range(2)]
    for pair in loads:
        for cp in pair:
            cp.start()
    ones = jnp.where(lax.broadcasted_iota(jnp.int32, (8, 128), 0) == 0, 1.0, 0.0).astype(F32)
    for q in range(N_REP):
        rows = lax.dot_general(sq[q], ones, (((0,), (0,)), ((), ())),
                               precision=lax.Precision.HIGHEST, preferred_element_type=F32)
        norm[q * 128:(q + 1) * 128, :] = jnp.sqrt(rows)

    for half in range(2):
        for cp in loads[half]:
            cp.wait()
        entries = buf.at[half].reshape(N_REP * 128, *HALF)

        def line(i, carry, half=half, entries=entries):
            for q in range(N_REP):
                for j in range(QCOL):
                    b = i * COLB + q * QCOL + j
                    scale = norm[pl.ds(q * 128 + i * QCOL + j, 1), :]
                    res[half, b] = (entries[tab[POS, b]].astype(F32) * scale).astype(BF)
            mine = pl.ds(i * COLB, COLB)
            pltpu.make_async_copy(res.at[half, mine], out.at[mine, half], left.at[half]).start()
            return carry

        lax.fori_loop(0, NBLK // COLB, line, 0)
    for half in range(2):
        pltpu.make_async_copy(res.at[half], out.at[:, half], left.at[half]).wait()


def tables(owners, tab):
    row = owners[...].reshape(1, NBLK)
    sub = lax.broadcasted_iota(jnp.int32, (NBLK, NBLK), 0)
    lane = lax.broadcasted_iota(jnp.int32, (NBLK, NBLK), 1)

    def down(mask, value=1):
        return jnp.sum(jnp.where(mask, value, 0), axis=0, keepdims=True)

    def along(mask, value=1):
        return jnp.sum(jnp.where(mask, value, 0), axis=1, keepdims=True)

    col = along(sub == lane, row)
    same = col == row
    slot_c = along(same & (lane < sub))
    slot_r = down(same & (sub < lane))
    key_c, key_r = slot_c * N_FSDP + col, slot_r * N_FSDP + row
    alike = (slot_c & 3) == (slot_r & 3)
    rank_c = along(alike & (slot_r >= 4) & (key_r < key_c))
    rank_r = down(alike & (slot_c >= 4) & (key_c < key_r))
    code = jnp.where(slot_c < 4, key_c, 1024 + (slot_c & 3) * PACKED + rank_c)
    e = lax.broadcasted_iota(jnp.int32, (1, 256), 1)
    block = lax.broadcasted_iota(jnp.int32, (NBLK, 1), 0)
    a = e - 128
    line = sum(jnp.where(a >= QCOL * i, 1, 0) for i in range(1, 8))
    for t in range(N_REP):
        want = jnp.where(e < 64, 1024 + t * PACKED + e, t * N_FSDP + e - 64)
        found = down(code == want, block)
        mine = line * COLB + t * QCOL + a - line * QCOL
        tab[t:t + 1, 0:256] = jnp.where(e < 128, found, jnp.where(e < LIST, mine, 0))
    for s in (1, 2):
        tab[RANK + s - 1:RANK + s, 0:256] = down(key_c == s * 256 + e, rank_c)
    tab[WHO:WHO + 1, 0:256] = down(code == 1024 + e, ((slot_c >> 2) - 1) * N_FSDP + col)
    tab[POS:POS + 1, 0:NBLK] = (slot_r & 3) * 128 + jnp.where(slot_r < 4, row, 64 + rank_r)


def shards(gradients, second_moment, left_roots, right_roots, owners):
    grads = gradients.reshape(8, 8, 160, 128).transpose(0, 2, 1, 3).reshape(NBLK, 2, *HALF)
    second = second_moment.reshape(8, 8, 40, 128).transpose(0, 2, 1, 3).reshape(80, 32, 128)
    left = left_roots.reshape(SLOTS, 512, 512)
    right = right_roots.reshape(SLOTS, 512, 512)
    smem = pl.BlockSpec(memory_space=pltpu.SMEM)
    vmem = pl.BlockSpec(memory_space=pltpu.VMEM)
    hbm = pl.BlockSpec(memory_space=pl.ANY)
    dma = pltpu.SemaphoreType.DMA
    vm = pltpu.VMEM
    tab = pl.pallas_call(
        tables,
        out_shape=jax.ShapeDtypeStruct((8, 384), jnp.int32),
        in_specs=[vmem],
        out_specs=vmem,
        name="tables",
    )(owners)
    ag, sq = pl.pallas_call(
        exchange,
        out_shape=(
            jax.ShapeDtypeStruct((N_REP, PARTS, 64, *HALF), BF),
            jax.ShapeDtypeStruct((N_REP, 8, 128), F32),
        ),
        in_specs=[smem, hbm, hbm, hbm, hbm],
        out_specs=(hbm, vmem),
        scratch_shapes=[
            vm((NBLK, 2, *HALF), BF), vm((ENTRIES, *HALF), BF), vm((ENTRIES, *HALF), BF),
            vm((2, ENTRIES, *HALF), BF), vm((2, ENTRIES, *HALF), BF),
            vm((2, PACKED, *HALF), BF), vm((2, PACKED, *HALF), BF),
            vm((SLOTS, 2, N_FSDP, *HALF), BF), vm((SLOTS, 2, N_FSDP, *HALF), BF),
            vm((512, 512), F32), vm((512, 512), BF),
            vm((SLOTS, 512, 512), F32), vm((SLOTS, 512, 512), F32),
            vm((SLOTS, 512, 512), BF), vm((SLOTS, 512, 512), BF),
            vm((SLOTS, 512, 512), BF), vm((SLOTS, 512, 512), BF), vm((80, 32, 128), F32),
            vm((SLOTS, 512, 512), F32), vm((SLOTS, 2, N_FSDP, *HALF), BF),
            vm((2, N_FSDP, *HALF), BF), vm((2, N_FSDP, *HALF), BF), vm((2, PACKED, *HALF), BF), vm((128, 128), F32),
            vm((8, 128), F32), vm((8, 128), F32), vm((8, 128), F32),
            vm((8, 8, 128), F32), vm((8, 8, 128), F32), vm((N_REP, 8, 128), F32),
            dma((3,)), dma((len(CHUNKS), 2)),
            dma((SLOTS, 2)), dma((SLOTS, 2)), dma((SLOTS, 2)), dma((SLOTS, 2)),
            dma((PARTS,)), dma((PARTS, 3)), dma((3,)), dma((3,)), dma((12,)), pltpu.SemaphoreType.REGULAR,
        ],
        compiler_params=pltpu.CompilerParams(collective_id=0, has_side_effects=True, vmem_limit_bytes=VMEM_LIMIT),
        name="exchange",
    )(tab, grads, second, left, right)
    out = pl.pallas_call(
        place,
        out_shape=jax.ShapeDtypeStruct((NBLK, 2, *HALF), BF),
        in_specs=[smem, hbm, vmem],
        out_specs=hbm,
        scratch_shapes=[vm((N_REP * 128, 128), F32), vm((2, N_REP, 2, 64, *HALF), BF), vm((2, NBLK, *HALF), BF),
                        dma((2, 2)), dma((2,))],
        compiler_params=pltpu.CompilerParams(vmem_limit_bytes=VMEM_LIMIT),
        name="place",
    )(tab, ag, sq)
    return out.reshape(8, 160, 8, 128).transpose(0, 2, 1, 3).reshape(8, 8, 20480)


def solution(mesh):
    return jax.shard_map(
        shards,
        mesh=mesh,
        in_specs=(
            P("rep", None, "fsdp", None),
            P(None, "fsdp", "rep"),
            P("fsdp", None, "rep", None, None),
            P("fsdp", None, "rep", None, None),
            P(),
        ),
        out_specs=P(None, "fsdp", None),
        check_vma=False,
    )
```
